256 devices in a mesh: tok: 64 (over x, z, core), feat: 4 (over y).
Axes of the slice: x: 4, y: 4, z: 8, core: 2. Of those that a mesh axis runs over, the one named last changes fastest.
Arguments:
- earlier: bfloat16 [65536, 6144], P('tok', 'feat'), may hold values from -6 to 6
- window_x: bfloat16 [65536, 2048], P(('tok', 'feat')), may hold values from -6 to 6
- off_block: bfloat16 [2048, 6144], P('tok', 'feat'), may hold values from -0.078125 to 0.078125
- diag_block: bfloat16 [2048, 2048], P(('tok', 'feat')), as said below
Outputs:
- whitened: float32 [65536, 2048], P(('tok', 'feat'))
The draws below stay inside these ranges and needn't reach their ends.
Inputs may be any that keep to these rules, and one draw needn't show every extreme that they name: diag_block is lower triangular with diagonal entries between 1 and 3.
All inputs are finite; a program needn't handle non-finite values.
Results may differ from the reference program's by a relative error of at most 0.0003.
Values may be sent and summed in bfloat16 or wider, within the bound.
A program may use at most 128 MiB of HBM per device.

```python
import jax
import jax.numpy as jnp
from jax import lax

WIN = 2048
K = 6144
TOKENS = 65536


def lower_factor(noise, diagonal, strength):
    rate = 8.0 / WIN
    spread = (strength * (jnp.exp(2.0 * rate) - 1.0)) ** 0.5
    row_index = jnp.arange(WIN)[:, None]
    col_index = jnp.arange(WIN)[None, :]
    distance = (row_index - col_index).astype(jnp.float32)
    decay = jnp.exp(-jnp.maximum(distance, 0.0) * rate)
    strict = jnp.where(row_index > col_index, noise * decay * spread, 0.0)
    return strict + jnp.where(row_index == col_index, diagonal[:, None], 0.0)


def draw_diag_block(key, part):
    key = jax.random.fold_in(key, 5)
    first_key, second_key = jax.random.split(key)
    noise = jax.random.normal(first_key, (WIN, WIN), jnp.float32)
    diagonal = jax.random.uniform(second_key, (WIN,), jnp.float32, 1.0, 2.0)
    return lower_factor(noise, diagonal, 1.2).astype(jnp.bfloat16)


def shard_levels(key, extent, cuts, least, largest):
    loudness, own = 1.0, jax.random.fold_in(key, 6)
    for dim, blocks in cuts:
        draws = jnp.exp(jax.random.uniform(jax.random.fold_in(own, dim), (blocks,), jnp.float32, least / len(cuts), largest / len(cuts)))
        loudness = loudness * jnp.repeat(draws, extent[dim] // blocks).reshape([-1 if axis == dim else 1 for axis in range(len(extent))])
    return loudness


def centred(stream_key, extent, deviation, bound, cuts=(), dtype=jnp.bfloat16):
    array = jax.random.normal(stream_key, extent, jnp.float32) * deviation
    if len(cuts) > 0:
        array = shard_levels(stream_key, extent, cuts, -0.22, 0.18) * array
    return jnp.clip(array, min=-bound, max=bound).astype(dtype)


def setup_inputs(seed: int = 0) -> dict:
    streams_of = jax.random.split(jax.random.key(seed), 5)
    return {
        "earlier": centred(streams_of[0], (TOKENS, K), 1.0, 6.0, ((0, 64), (1, 4))),
        "window_x": centred(streams_of[1], (TOKENS, WIN), 1.0, 6.0, ((0, 256),)),
        "off_block": centred(streams_of[2], (WIN, K), K ** -0.5, 0.078125, ((0, 64), (1, 4))),
        "diag_block": draw_diag_block(jax.random.fold_in(streams_of[4], 71), 0),
    }


def solve_right(lower, values):
    return lax.linalg.triangular_solve(lower, values, left_side=False, lower=True, transpose_a=True)

def solve_panels(remainder, lower):
    width = lower.shape[0] // 2
    first = solve_right(lower[:width, :width], remainder[:, :width])
    rest = remainder[:, width:] - jnp.dot(first.astype(jnp.float32), lower[width:, :width].T.astype(jnp.float32), precision=lax.Precision.HIGHEST, preferred_element_type=jnp.float32)
    second = solve_right(lower[width:, width:], rest)
    return jnp.concatenate([first, second], axis=1)

def reference(earlier, window_x, off_block, diag_block):
    update = jnp.dot(earlier.astype(jnp.float32), off_block.T.astype(jnp.float32), preferred_element_type=jnp.float32)
    remainder = window_x.astype(jnp.float32) - update
    return solve_panels(remainder, diag_block.astype(jnp.float32))
```

```python
import jax
import jax.numpy as jnp
from jax import lax
from jax.experimental import pallas as pl
from jax.experimental.pallas import tpu as pltpu
from jax.sharding import PartitionSpec as P

f32, bf16 = jnp.float32, jnp.bfloat16
NX, NY, NZ = 4, 4, 8
WIN, COLS, ROWS, TOK = 2048, 1536, 32, 256
CHUNKS, CW = 16, 128
LAG = 3
FLOOR = 2.0**-10


def split(v):
    high = v.astype(bf16)
    return high, (v - high.astype(f32)).astype(bf16)


def dot(a, b):
    return lax.dot_general(a, b, (((1,), (0,)), ((), ())), preferred_element_type=f32)


def dot_t(a, b):
    return lax.dot_general(a, b, (((1,), (1,)), ((), ())), preferred_element_type=f32)


def dot3(a, b):
    ah, al = split(a)
    bh, bl = split(b)
    return dot(ah, bh) + (dot(ah, bl) + dot(al, bh))


def encode(v):
    m = jnp.abs(v) + FLOOR
    m2 = m * m
    m4 = m2 * m2
    m12 = m4 * m4 * m4
    return jnp.where(v < 0, -m12, m12).astype(bf16)


def decode(code):
    c = code.astype(f32)
    m = jnp.exp(jnp.log(jnp.abs(c)) * (1.0 / 12.0)) - FLOOR
    return jnp.where(c < 0, -m, m)


def inverse(block):
    n = block.shape[0]
    r = lax.broadcasted_iota(jnp.int32, (n, n), 0)
    c = lax.broadcasted_iota(jnp.int32, (n, n), 1)
    differ = r ^ c
    x = jnp.where(differ == 0, 1.0 / jnp.where(differ == 0, block, 1.0), 0.0)
    s = 1
    while s < n:
        below = jnp.where((differ >= s) & (differ < 2 * s), block, 0.0).astype(bf16)
        xh, xl = split(x)
        th, tl = split(dot(xh, below) + dot(xl, below))
        x = x - (dot(th, xh) + (dot(th, xl) + dot(tl, xh)))
        s *= 2
    return x


def kept(xb):
    return 512 * xb + 256


def kernel(e, xw, w, dg, out, wb, db, lb, hs, si, sd, hr, gi, gd, pb, pk, rem, ih, il, acc,
           wz_s, wz_r, wx_s, wx_r, wf_s, ws_s, ws_r, dy_s, dy_r, dx_s, dx_r, dz_s, dz_r, ds_s, ds_r,
           ly_s, ly_r, lx_s, lx_r, lz_s, lz_r, ls_s, ls_r, rs_s, rs_r, in_s, in_r):
    t, y = lax.axis_index("tok"), lax.axis_index("feat")
    x, z, c = lax.div(t, 16), lax.rem(lax.div(t, 2), 8), lax.rem(t, 2)

    def at(dx=0, dy=0, dz=0, dc=0):
        xx, yy = lax.rem(x + dx + NX, NX), lax.rem(y + dy + NY, NY)
        zz, cc = lax.rem(z + dz + NZ, NZ), lax.rem(c + dc, 2)
        return (xx * 16 + zz * 2 + cc, yy)

    def copy(src, ss, rs, device, dst=None):
        return pltpu.make_async_remote_copy(
            src_ref=src, dst_ref=src if dst is None else dst, send_sem=ss, recv_sem=rs,
            device_id=device, device_id_type=pl.DeviceIdType.MESH)

    east, west, up, down, twin = at(dx=1), at(dx=-1), at(dz=1), at(dz=-1), at(dc=1)
    sides = [at(dx=d) for d in (1, 2, 3)]
    others = [at(dy=d) for d in (1, 2, 3)]

    wb[x, z, c] = w[...]
    lb[x, z, c, y] = dg[...]
    db[x, z, c, y] = dg[:, pl.ds(pl.multiple_of((2 * x + lax.div(z, 4)) * 256, 256), 256)]

    barrier = pltpu.get_barrier_semaphore()
    partners = [up, down, twin, *sides, *others]
    for p in partners:
        pl.semaphore_signal(barrier, inc=1, device_id=p, device_id_type=pl.DeviceIdType.MESH)
    pl.semaphore_wait(barrier, len(partners))

    sg = 2 * lax.rem(z, 2) - 1

    def pair_of(k):
        off = jnp.where(k == 0, 0, jnp.where(k == 1, sg, jnp.where(k == 2, -sg, 2)))
        return lax.rem(lax.div(z, 2) + off + 4, 4)

    def chunk_of(s):
        near = jnp.logical_and(s >= 4, s < 12)
        k = jnp.where(s < 4, s, jnp.where(near, lax.div(s - 4, 2), s - 12))
        side = lax.rem(s, 2)
        xs = jnp.where(s < 4, x, jnp.where(near, x + 3 + 2 * side, x + 2))
        return lax.rem(xs, NX), pair_of(k)

    def rows_of(xs, pair, core):
        return wb.at[xs, pl.ds(2 * pair, 2), core]

    def w_ring(k, zsrc, way):
        return copy(wb.at[x, zsrc, c], wz_s.at[way, k], wz_r.at[zsrc], up if way == 0 else down)

    def w_side(s, way):
        return copy(rows_of(x, pair_of(s), c), wx_s.at[way, s], wx_r.at[way, s], east if way == 0 else west)

    def w_far(k, side, xs):
        return copy(rows_of(xs, pair_of(k), c), wf_s.at[k], wx_r.at[2, k], at(dx=1 - 2 * side))

    def w_twin(s, core):
        xs, pair = chunk_of(s)
        return copy(rows_of(xs, pair, core), ws_s.at[s], ws_r.at[s], twin)

    def w_step(s):
        @pl.when(s < 4)
        def _():
            k = s + 1
            zm, zp = lax.rem(z - k + NZ, NZ), lax.rem(z + k, NZ)
            w_ring(0, zm, 0).wait_recv()

            @pl.when(k < 4)
            def _():
                w_ring(k, zm, 0).start()
                w_ring(0, zp, 1).wait_recv()

            @pl.when(k < 3)
            def _():
                w_ring(k, zp, 1).start()

            w_twin(s, c).start()
            w_side(s, 0).start()
            w_side(s, 1).start()

        @pl.when(jnp.logical_and(s >= 4, s < 12))
        def _():
            k, side = lax.div(s - 4, 2), lax.rem(s, 2)
            xs = lax.rem(x + 3 + 2 * side, NX)
            pair = pair_of(k)
            copy(rows_of(xs, pair, c), wx_s.at[0, 0], wx_r.at[side, k], twin).wait_recv()
            w_twin(s, c).start()

            @pl.when(lax.rem(k, 2) == side)
            def _():
                w_far(k, side, xs).start()

        @pl.when(jnp.logical_and(s >= 12, s < CHUNKS))
        def _():
            k = s - 12
            copy(rows_of(lax.rem(x + 2, NX), pair_of(k), c), wx_s.at[0, 0], wx_r.at[2, k], twin).wait_recv()
            w_twin(s, c).start()

    def d_y(d, yy):
        return copy(db.at[x, z, c, yy], dy_s.at[d], dy_r.at[d], others[d])

    def l_y(d, yy):
        return copy(lb.at[x, z, c, yy], ly_s.at[d], ly_r.at[d], others[d])

    def d_x(d, xx):
        return copy(db.at[xx, z, c], dx_s.at[d], dx_r.at[d], sides[d])

    def l_x(d, xx):
        return copy(lb.at[xx, z, c], lx_s.at[d], lx_r.at[d], sides[d])

    def d_ring(k, zsrc, way):
        return copy(db.at[:, zsrc, c], dz_s.at[way, k], dz_r.at[zsrc], up if way == 0 else down)

    def d_twin(zsrc, core):
        return copy(db.at[:, zsrc, core], ds_s.at[zsrc], ds_r.at[zsrc], twin)

    def l_rows(xb, zsrc, core):
        return lb.at[xb, zsrc, core, :, :, pl.ds(0, kept(xb))]

    def l_ring(k, xb, zsrc, way):
        return copy(l_rows(xb, zsrc, c), lz_s.at[way, k, xb], lz_r.at[zsrc, xb], up if way == 0 else down)

    def l_twin(xb, zsrc, core):
        return copy(l_rows(xb, zsrc, core), ls_s.at[zsrc, xb], ls_r.at[zsrc, xb], twin)

    UPPER, LOWER = (0, 3), (1, 2)

    def l_step(k):
        zm, zp = lax.rem(z - k + NZ, NZ), lax.rem(z + k, NZ)
        for xb in range(NX):
            l_ring(0, xb, zm, 0).wait_recv()
            if k < 3 or (k == 3 and xb in UPPER):
                l_ring(k, xb, zm, 0).start()
            l_twin(xb, zm, c).start()
            if k < 4:
                l_ring(0, xb, zp, 1).wait_recv()
                if k < 3 or xb in LOWER:
                    l_ring(k, xb, zp, 1).start()
                l_twin(xb, zp, c).start()

    def factor_step(s):
        @pl.when(s == 0)
        def _():
            for d in range(3):
                d_y(d, lax.rem(y + 3 - d, NY)).wait_recv()
            for d in range(3):
                d_x(d, x).start()
            for d in range(3):
                l_y(d, lax.rem(y + 3 - d, NY)).wait_recv()
            for d in range(3):
                l_x(d, x).start()

        @pl.when(s == 1)
        def _():
            for d in range(3):
                d_x(d, lax.rem(x + 3 - d, NX)).wait_recv()
            d_ring(0, z, 0).start()
            d_ring(0, z, 1).start()
            d_twin(z, c).start()
            for d in range(3):
                l_x(d, lax.rem(x + 3 - d, NX)).wait_recv()
            for xb in range(NX):
                l_ring(0, xb, z, 0).start()
                l_ring(0, xb, z, 1).start()
                l_twin(xb, z, c).start()

        @pl.when(jnp.logical_and(s >= 2, s < 6))
        def _():
            k = s - 1
            zm, zp = lax.rem(z - k + NZ, NZ), lax.rem(z + k, NZ)
            d_ring(0, zm, 0).wait_recv()

            @pl.when(k < 4)
            def _():
                d_ring(k, zm, 0).start()
                d_ring(0, zp, 1).wait_recv()
                d_twin(zp, c).start()

            @pl.when(k < 3)
            def _():
                d_ring(k, zp, 1).start()

            d_twin(zm, c).start()

        @pl.when(s == 6)
        def _():
            for zz in range(NZ):
                d_twin(zz, 1 - c).wait_recv()

        for k, when in ((1, 5), (2, 8), (3, 11), (4, 14)):

            @pl.when(s == when)
            def _(k=k):
                l_step(k)

    def inverse_copies(i, core):
        j = 2 * i + core
        return (copy(ih.at[j], in_s.at[0, i], in_r.at[0, i], twin), copy(il.at[j], in_s.at[1, i], in_r.at[1, i], twin))

    def inverse_step(s):
        @pl.when(jnp.logical_and(s >= 8, lax.rem(s, 2) == 0) & (s < 16))
        def _():
            i = lax.div(s - 8, 2)
            j = 2 * i + c
            block = db[i, pl.ds(4 * c, 4)].reshape(256, 256).astype(f32)
            a, d = inverse(block[:128, :128]), inverse(block[128:, 128:])
            below = block[128:, :128].astype(bf16)
            dh, dl = split(d)
            b = -dot3(dot(dh, below) + dot(dl, below), a)
            for rows, cols, v in ((0, 0, a), (1, 1, d), (1, 0, b), (0, 1, jnp.zeros_like(a))):
                vh, vl = split(v)
                ih[j, pl.ds(128 * rows, 128), pl.ds(128 * cols, 128)] = vh
                il[j, pl.ds(128 * rows, 128), pl.ds(128 * cols, 128)] = vl
            for cp in inverse_copies(i, c):
                cp.start()

    def toward(s):
        return lax.rem(y + 1 + 2 * lax.rem(s, 2), NY)

    def share(n, s):
        to = toward(s) if n != 1 else lax.rem(toward(s) + 2, NY)
        src, dst = ((hs, hr), (si, gi), (sd, gd))[n]
        return copy(src.at[s], rs_s.at[n, s], rs_r.at[n, s], (t, to), dst.at[s])

    def multiply(s):
        xs, pair = chunk_of(s)
        w_twin(s, 1 - c).wait_recv()
        rows = wb[xs, pl.ds(2 * pair, 2)].reshape(CW, COLS)
        pb[...] = dot_t(e[...], rows)

        def part(d):
            return pb[pl.ds(pl.multiple_of(d * TOK, TOK), TOK), :]

        nd = toward(s)
        hs[s] = encode(part(lax.rem(y + 2, NY)))
        share(0, s).start()
        si[s] = encode(part(lax.rem(nd + 2, NY)))
        share(1, s).start()
        pk[lax.rem(s, 2)] = part(nd)
        q = 4 * xs + pair
        rem[q] = xw[:, pl.ds(pl.multiple_of(q * CW, CW), CW)].astype(f32) - part(y)

    def pass_on(s):
        share(0, s).wait_recv()
        sd[s] = encode(pk[lax.rem(s, 2)] + decode(hr[s]))
        share(2, s).start()

    def finish(s):
        xs, pair = chunk_of(s)
        q = 4 * xs + pair
        share(1, s).wait_recv()
        share(2, s).wait_recv()
        rem[q] = rem[q] - (decode(gi[s]) + decode(gd[s]))

    w_ring(0, z, 0).start()
    w_ring(0, z, 1).start()
    for d in range(3):
        d_y(d, y).start()
    for d in range(3):
        l_y(d, y).start()
    w_step(jnp.int32(0))

    @pl.loop(0, CHUNKS + LAG)
    def _(s):
        @pl.when(s < CHUNKS)
        def _():
            multiply(s)

        @pl.when(s + 1 < CHUNKS)
        def _():
            w_step(s + 1)

        factor_step(s)

        @pl.when(jnp.logical_and(s >= 1, s <= CHUNKS))
        def _():
            pass_on(s - 1)

        inverse_step(s)

        @pl.when(s >= LAG)
        def _():
            finish(s - LAG)

    for zz in range(NZ):
        for xb in range(NX):
            l_twin(xb, zz, 1 - c).wait_recv()
    for i in range(4):
        for cp in inverse_copies(i, 1 - c):
            cp.wait_recv()

    for j in range(8):
        v = jnp.concatenate([rem[2 * j], rem[2 * j + 1]], axis=1)
        if j:
            v = v - acc[j]
        vh, vl = split(v)
        o = dot_t(vh, ih[j]) + (dot_t(vh, il[j]) + dot_t(vl, ih[j]))
        out[:, 256 * j : 256 * j + 256] = o
        oh, ol = split(o)
        for i in range(j + 1, 8):
            block = lb[i // 2, pl.ds(4 * (i % 2), 4), :, :, :, pl.ds(256 * j, 256)].reshape(256, 256)
            u = dot_t(oh, block) + dot_t(ol, block)
            acc[i] = u if j == 0 else acc[i] + u

    for k in range(4):
        w_ring(k, z, 0).wait_send()
        if k < 3:
            w_ring(k, z, 1).wait_send()
        w_side(k, 0).wait_send()
        w_side(k, 1).wait_send()
        w_far(k, 0, x).wait_send()
    for s in range(CHUNKS):
        w_twin(s, c).wait_send()
        for n in range(3):
            share(n, s).wait_send()
    for d in range(3):
        for cp in (d_y(d, y), l_y(d, y), d_x(d, x), l_x(d, x)):
            cp.wait_send()
    for k in range(4):
        d_ring(k, z, 0).wait_send()
        if k < 3:
            d_ring(k, z, 1).wait_send()
        for xb in range(NX):
            if k < 3 or xb in UPPER:
                l_ring(k, xb, z, 0).wait_send()
            if k < 3 or xb in LOWER:
                l_ring(k, xb, z, 1).wait_send()
    for zz in range(NZ):
        d_twin(zz, c).wait_send()
        for xb in range(NX):
            l_twin(xb, zz, c).wait_send()
    for i in range(4):
        for cp in inverse_copies(i, c):
            cp.wait_send()


def local(earlier, window_x, off_block, diag_block):
    V, D = pltpu.VMEM, pltpu.SemaphoreType.DMA
    msg = V((CHUNKS, TOK, CW), bf16)
    scratch = [
        V((NX, NZ, 2, ROWS, COLS), bf16),
        V((NX, NZ, 2, NY, 8, 256), bf16),
        V((NX, NZ, 2, NY, 8, WIN), bf16),
        msg, msg, msg, msg, msg, msg,
        V((4 * TOK, CW), f32),
        V((2, TOK, CW), f32),
        V((CHUNKS, TOK, CW), f32),
        V((8, 256, 256), bf16),
        V((8, 256, 256), bf16),
        V((8, TOK, 256), f32),
        D((2, 4)), D((8,)), D((2, 4)), D((3, 4)), D((4,)), D((CHUNKS,)), D((CHUNKS,)),
        D((3,)), D((3,)), D((3,)), D((3,)), D((2, 4)), D((8,)), D((8,)), D((8,)),
        D((3,)), D((3,)), D((3,)), D((3,)), D((2, 4, 4)), D((8, 4)), D((8, 4)), D((8, 4)),
        D((3, CHUNKS)), D((3, CHUNKS)), D((2, 4)), D((2, 4)),
    ]
    return pl.pallas_call(
        kernel,
        out_shape=jax.ShapeDtypeStruct((TOK, WIN), f32),
        in_specs=[pl.BlockSpec(memory_space=pltpu.VMEM)] * 4,
        out_specs=pl.BlockSpec(memory_space=pltpu.VMEM),
        scratch_shapes=scratch,
        name="whiten",
        compiler_params=pltpu.CompilerParams(
            collective_id=0, has_side_effects=True, vmem_limit_bytes=56 * 2**20
        ),
    )(earlier, window_x, off_block, diag_block)


def solution(mesh):
    return jax.shard_map(
        local,
        mesh=mesh,
        in_specs=(
            P("tok", "feat"),
            P(("tok", "feat"), None),
            P("tok", "feat"),
            P(("tok", "feat"), None),
        ),
        out_specs=P(("tok", "feat"), None),
        check_vma=False,
    )
```

```python
import jax
import jax.numpy as jnp
from jax import lax
from jax.experimental import pallas as pl
from jax.experimental.pallas import tpu as pltpu
from jax.sharding import PartitionSpec as P

f32, bf16 = jnp.float32, jnp.bfloat16
NX, NY, NZ = 4, 4, 8
WIN, COLS, ROWS, TOK = 2048, 1536, 32, 256
CHUNKS, CW = 16, 128
TICKS = 9
FLOOR = 2.0**-10


def split(v):
    high = v.astype(bf16)
    return high, (v - high.astype(f32)).astype(bf16)


def dot(a, b):
    return lax.dot_general(a, b, (((1,), (0,)), ((), ())), preferred_element_type=f32)


def dot_t(a, b):
    return lax.dot_general(a, b, (((1,), (1,)), ((), ())), preferred_element_type=f32)


def encode(v):
    m = jnp.abs(v) + FLOOR
    m2 = m * m
    m4 = m2 * m2
    m12 = m4 * m4 * m4
    return jnp.where(v < 0, -m12, m12).astype(bf16)


def decode(code):
    c = code.astype(f32)
    m = jnp.exp(jnp.log(jnp.abs(c)) * (1.0 / 12.0)) - FLOOR
    return jnp.where(c < 0, -m, m)


def inverse(block):
    n = block.shape[0]
    r = lax.broadcasted_iota(jnp.int32, (n, n), 0)
    c = lax.broadcasted_iota(jnp.int32, (n, n), 1)
    differ = r ^ c
    x = jnp.where(differ == 0, 1.0 / jnp.where(differ == 0, block, 1.0), 0.0)
    s = 1
    while s < n:
        below = jnp.where((differ >= s) & (differ < 2 * s), block, 0.0).astype(bf16)
        xh, xl = split(x)
        th, tl = split(dot(xh, below) + dot(xl, below))
        x = x - (dot(th, xh) + (dot(th, xl) + dot(tl, xh)))
        s *= 2
    return x


def kept(xb):
    return 512 * xb + 384


def kernel(e_hbm, x_hbm, w, dg, out_hbm, e, xw, ov, wb, gb, iv, vb, lb, hs, si, sd, hr, gi, gd, pb, pk, rem, ih, il, acc,
           in_s, out_s, wz_s, wz_r, wx_s, wx_r, wf_s, ws_s, ws_r, gy_s, gy_r, gg_s, gg_r, vx_s, vx_r, vz_s, vz_r, vt_s, vt_r,
           lx_s, lx_r, ly_s, ly_r, lz_s, lz_r, lt_s, lt_r, rs_s, rs_r):
    t, y = lax.axis_index("tok"), lax.axis_index("feat")
    x, z, c = lax.div(t, 16), lax.rem(lax.div(t, 2), 8), lax.rem(t, 2)
    low = lax.rem(z, 2)

    def at(dx=0, dy=0, dz=0, dc=0):
        xx, yy = lax.rem(x + dx + NX, NX), lax.rem(y + dy + NY, NY)
        zz, cc = lax.rem(z + dz + NZ, NZ), lax.rem(c + dc, 2)
        return (xx * 16 + zz * 2 + cc, yy)

    def copy(src, ss, rs, device, dst=None):
        return pltpu.make_async_remote_copy(
            src_ref=src, dst_ref=src if dst is None else dst, send_sem=ss, recv_sem=rs,
            device_id=device, device_id_type=pl.DeviceIdType.MESH)

    load_e = pltpu.make_async_copy(e_hbm, e, in_s.at[0])
    load_x = pltpu.make_async_copy(x_hbm, xw, in_s.at[1])
    load_e.start()
    load_x.start()

    east, west, up, down, twin = at(dx=1), at(dx=-1), at(dz=1), at(dz=-1), at(dc=1)
    mates = [twin, at(dz=1 - 2 * low), at(dz=1 - 2 * low, dc=1)]
    sides = [at(dx=d) for d in (1, 2, 3)]
    others = [at(dy=d) for d in (1, 2, 3)]

    wb[x, z, c] = w[...]
    lb[x, z, c, y] = dg[...]
    gb[low, c, y] = dg[:, pl.ds(pl.multiple_of(lax.div(t, 4) * 128, 128), 128)]

    barrier = pltpu.get_barrier_semaphore()
    partners = [up, down, twin, mates[2], *sides, *others]
    for p in partners:
        pl.semaphore_signal(barrier, inc=1, device_id=p, device_id_type=pl.DeviceIdType.MESH)
    pl.semaphore_wait(barrier, len(partners))

    sg = 2 * low - 1

    def pair_of(k):
        off = jnp.where(k == 0, 0, jnp.where(k == 1, sg, jnp.where(k == 2, -sg, 2)))
        return lax.rem(lax.div(z, 2) + off + 4, 4)

    def chunk_of(n):
        side, g = lax.rem(n, 2), lax.div(n, 2)
        own = jnp.logical_or(g == 0, g == 3)
        far = g >= 6
        near_k = jnp.where(g < 3, g - 1, g - 2)
        k = jnp.where(own, jnp.where(g == 0, side, 2 + side), jnp.where(far, n - 12, near_k))
        xs = jnp.where(own, x, jnp.where(far, x + 2, x + 3 + 2 * side))
        return lax.rem(xs, NX), pair_of(k)

    def rows_of(xs, pair, core):
        return wb.at[xs, pl.ds(2 * pair, 2), core]

    def w_ring(k, zsrc, way):
        return copy(wb.at[x, zsrc, c], wz_s.at[way, k], wz_r.at[zsrc], up if way == 0 else down)

    def w_side(k, way):
        return copy(rows_of(x, pair_of(k), c), wx_s.at[way, k], wx_r.at[way, k], east if way == 0 else west)

    def w_near(k, side):
        return copy(rows_of(lax.rem(x + 3 + 2 * side, NX), pair_of(k), c), wf_s.at[k], wx_r.at[side, k], twin)

    def w_on(k):
        side = k % 2
        return copy(rows_of(lax.rem(x + 3 + 2 * side, NX), pair_of(k), c), wf_s.at[k], wx_r.at[2, k], (east, west)[side])

    def w_far(k):
        return copy(rows_of(lax.rem(x + 2, NX), pair_of(k), c), wf_s.at[k], wx_r.at[2, k], twin)

    def w_twin(n, core):
        xs, pair = chunk_of(n)
        return copy(rows_of(xs, pair, core), ws_s.at[n], ws_r.at[n], twin)

    def own_step(k):
        zm, zp = lax.rem(z - (k + 1) + NZ, NZ), lax.rem(z + k + 1, NZ)
        w_ring(0, zm, 0).wait_recv()
        if k < 3:
            w_ring(k + 1, zm, 0).start()
            w_ring(0, zp, 1).wait_recv()
        if k < 2:
            w_ring(k + 1, zp, 1).start()
        w_twin(jnp.int32((0, 1, 6, 7)[k]), c).start()
        w_side(k, 0).start()
        w_side(k, 1).start()

    def near_step(k):
        for side in (0, 1):
            w_near(k, side).wait_recv()
            if side == k % 2:
                w_on(k).start()
            w_twin(jnp.int32((2, 4, 8, 10)[k] + side), c).start()

    def far_step(k):
        w_far(k).wait_recv()
        w_twin(jnp.int32(12 + k), c).start()

    def fetch(tick):
        @pl.when(tick == 0)
        def _():
            own_step(1)

        @pl.when(tick == 1)
        def _():
            own_step(2)
            near_step(0)

        @pl.when(tick == 2)
        def _():
            own_step(3)
            near_step(1)

        @pl.when(tick == 3)
        def _():
            near_step(2)

        @pl.when(tick == 5)
        def _():
            near_step(3)

        @pl.when(tick == 6)
        def _():
            far_step(0)
            far_step(1)

        @pl.when(tick == 7)
        def _():
            far_step(2)
            far_step(3)

    def g_y(d, yy):
        return copy(gb.at[low, c, yy], gy_s.at[d], gy_r.at[d], others[d])

    def g_mate(i, zl, core):
        return copy(gb.at[zl, core], gg_s.at[i], gg_r.at[i], mates[i])

    def v_x(d, xx):
        return copy(vb.at[xx, z, c], vx_s.at[d], vx_r.at[d], sides[d])

    def v_ring(k, zsrc, way):
        return copy(vb.at[:, zsrc, c], vz_s.at[way, k], vz_r.at[zsrc], up if way == 0 else down)

    def v_twin(zsrc, core):
        return copy(vb.at[:, zsrc, core], vt_s.at[zsrc], vt_r.at[zsrc], twin)

    def invert():
        g_mate(0, low, 1 - c).wait_recv()
        g_mate(1, 1 - low, c).wait_recv()
        g_mate(2, 1 - low, 1 - c).wait_recv()
        iv[0], iv[1] = split(inverse(gb[...].reshape(128, 128).astype(f32)))
        mine = pl.ds(pl.multiple_of(32 * (2 * low + c), 32), 32)
        vb[x, z, c, 0] = iv[0, mine]
        vb[x, z, c, 1] = iv[1, mine]
        for d in range(3):
            v_x(d, x).start()

    def v_step(k):
        if k == 0:
            for d in range(3):
                v_x(d, lax.rem(x + 3 - d, NX)).wait_recv()
            v_ring(0, z, 0).start()
            v_ring(0, z, 1).start()
            v_twin(z, c).start()
            return
        zm, zp = lax.rem(z - k + NZ, NZ), lax.rem(z + k, NZ)
        v_ring(0, zm, 0).wait_recv()
        if k < 4:
            v_ring(k, zm, 0).start()
            v_ring(0, zp, 1).wait_recv()
            if k < 3:
                v_ring(k, zp, 1).start()
            v_twin(zp, c).start()
        v_twin(zm, c).start()

    def l_x(d, xx):
        return copy(lb.at[xx, z, c, y], lx_s.at[d], lx_r.at[d], sides[d])

    def l_y(d, xb, yy):
        return copy(lb.at[xb, z, c, yy, :, pl.ds(0, kept(xb))], ly_s.at[d, xb], ly_r.at[d, xb], others[d])

    def l_rows(xb, zsrc, core):
        return lb.at[xb, zsrc, core, :, :, pl.ds(0, kept(xb))]

    def l_ring(k, xb, zsrc, way):
        return copy(l_rows(xb, zsrc, c), lz_s.at[way, k, xb], lz_r.at[zsrc, xb], up if way == 0 else down)

    def l_twin(xb, zsrc, core):
        return copy(l_rows(xb, zsrc, core), lt_s.at[zsrc, xb], lt_r.at[zsrc, xb], twin)

    UPPER, LOWER = (0, 3), (1, 2)

    def l_step(k):
        if k == 0:
            for xb in range(NX):
                for d in range(3):
                    l_y(d, xb, lax.rem(y + 3 - d, NY)).wait_recv()
                l_ring(0, xb, z, 0).start()
                l_ring(0, xb, z, 1).start()
                l_twin(xb, z, c).start()
            return
        zm, zp = lax.rem(z - k + NZ, NZ), lax.rem(z + k, NZ)
        for xb in range(NX):
            l_ring(0, xb, zm, 0).wait_recv()
            if k < 3 or (k == 3 and xb in UPPER):
                l_ring(k, xb, zm, 0).start()
            l_twin(xb, zm, c).start()
            if k < 4:
                l_ring(0, xb, zp, 1).wait_recv()
                if k < 3 or xb in LOWER:
                    l_ring(k, xb, zp, 1).start()
                l_twin(xb, zp, c).start()

    def join():
        for zz in range(NZ):
            v_twin(zz, 1 - c).wait_recv()
            for xb in range(NX):
                l_twin(xb, zz, 1 - c).wait_recv()
        for j in range(8):
            xb, first = j // 2, 4 * (j % 2)
            ah, al = (vb[xb, pl.ds(first, 2), :, h].reshape(128, 128) for h in (0, 1))
            dh, dl = (vb[xb, pl.ds(first + 2, 2), :, h].reshape(128, 128) for h in (0, 1))
            below = lb[xb, pl.ds(first + 2, 2), :, :, :, pl.ds(256 * j, 128)].reshape(128, 128)
            th, tl = split(dot(dh, below) + dot(dl, below))
            bh, bl = split(-(dot(th, ah) + (dot(th, al) + dot(tl, ah))))
            zero = jnp.zeros((128, 128), bf16)
            for ref, parts in ((ih, (ah, zero, bh, dh)), (il, (al, zero, bl, dl))):
                ref[j, :128, :128] = parts[0]
                ref[j, :128, 128:] = parts[1]
                ref[j, 128:, :128] = parts[2]
                ref[j, 128:, 128:] = parts[3]

    def factor(tick):
        @pl.when(tick == 0)
        def _():
            invert()

        @pl.when(tick == 1)
        def _():
            l_step(0)

        @pl.when(tick == 3)
        def _():
            v_step(0)

        @pl.when(tick == 4)
        def _():
            v_step(1)
            l_step(1)

        @pl.when(tick == 5)
        def _():
            v_step(2)

        @pl.when(tick == 6)
        def _():
            v_step(3)
            l_step(2)

        @pl.when(tick == 7)
        def _():
            v_step(4)

        @pl.when(tick == 8)
        def _():
            l_step(3)

        @pl.when(tick == 9)
        def _():
            l_step(4)
            join()

    def toward(n):
        return lax.rem(y + 1 + 2 * lax.rem(n, 2), NY)

    def share(kind, n):
        to = toward(n) if kind != 1 else lax.rem(toward(n) + 2, NY)
        src, dst = ((hs, hr), (si, gi), (sd, gd))[kind]
        return copy(src.at[n], rs_s.at[kind, n], rs_r.at[kind, n], (t, to), dst.at[n])

    def rows(n):
        xs, pair = chunk_of(n)
        w_twin(n, 1 - c).wait_recv()
        return wb[xs, pl.ds(2 * pair, 2)].reshape(CW, COLS)

    def hand_out(n, i):
        def part(d):
            return pb[pl.ds(pl.multiple_of(d * TOK, TOK), TOK), pl.ds(CW * i, CW)]

        nd = toward(n)
        hs[n] = encode(part(lax.rem(y + 2, NY)))
        share(0, n).start()
        si[n] = encode(part(lax.rem(nd + 2, NY)))
        share(1, n).start()
        pk[lax.rem(n, 4)] = part(nd)
        xs, pair = chunk_of(n)
        q = 4 * xs + pair
        rem[q] = xw[:, pl.ds(pl.multiple_of(q * CW, CW), CW)].astype(f32) - part(y)

    def pass_on(n):
        share(0, n).wait_recv()
        sd[n] = encode(pk[lax.rem(n, 4)] + decode(hr[n]))
        share(2, n).start()

    def finish(n):
        xs, pair = chunk_of(n)
        q = 4 * xs + pair
        share(1, n).wait_recv()
        share(2, n).wait_recv()
        rem[q] = rem[q] - (decode(gi[n]) + decode(gd[n]))

    def each(tick, do):
        n = jnp.where(tick < 2, tick, 2 * tick - 2)
        do(n)

        @pl.when(tick >= 2)
        def _():
            do(n + 1)

    w_ring(0, z, 0).start()
    w_ring(0, z, 1).start()
    for d in range(3):
        g_y(d, y).start()
    for d in range(3):
        l_x(d, x).start()
    own_step(0)
    for d in range(3):
        g_y(d, lax.rem(y + 3 - d, NY)).wait_recv()
    for i in range(3):
        g_mate(i, low, c).start()
    for d in range(3):
        l_x(d, lax.rem(x + 3 - d, NX)).wait_recv()
    for xb in range(NX):
        for d in range(3):
            l_y(d, xb, y).start()
    load_e.wait()
    load_x.wait()

    @pl.loop(0, TICKS + 2)
    def _(tick):
        @pl.when(tick < 2)
        def _():
            pb[:, pl.ds(0, CW)] = dot_t(e[...], rows(tick))
            hand_out(tick, 0)

        @pl.when(jnp.logical_and(tick >= 2, tick < TICKS))
        def _():
            n = 2 * tick - 2
            pb[...] = dot_t(e[...], jnp.concatenate([rows(n), rows(n + 1)], axis=0))
            hand_out(n, 0)
            hand_out(n + 1, 1)

        fetch(tick)

        @pl.when(jnp.logical_and(tick >= 1, tick <= TICKS))
        def _():
            each(tick - 1, pass_on)

        @pl.when(tick >= 2)
        def _():
            each(tick - 2, finish)

        factor(tick)

    def store(j):
        return pltpu.make_async_copy(ov.at[j], out_hbm.at[:, pl.ds(256 * j, 256)], out_s.at[j])

    for j in range(8):
        v = jnp.concatenate([rem[2 * j], rem[2 * j + 1]], axis=1)
        if j:
            v = v - acc[j]
        vh, vl = split(v)
        o = dot_t(vh, ih[j]) + (dot_t(vh, il[j]) + dot_t(vl, ih[j]))
        ov[j] = o
        store(j).start()
        oh, ol = split(o)
        for i in range(j + 1, 8):
            block = lb[i // 2, pl.ds(4 * (i % 2), 4), :, :, :, pl.ds(256 * j, 256)].reshape(256, 256)
            u = dot_t(oh, block) + dot_t(ol, block)
            acc[i] = u if j == 0 else acc[i] + u

    for k in range(4):
        w_ring(k, z, 0).wait_send()
        if k < 3:
            w_ring(k, z, 1).wait_send()
        w_side(k, 0).wait_send()
        w_side(k, 1).wait_send()
        w_on(k).wait_send()
    for n in range(CHUNKS):
        w_twin(n, c).wait_send()
        for kind in range(3):
            share(kind, n).wait_send()
    for d in range(3):
        for cp in (g_y(d, y), g_mate(d, low, c), v_x(d, x), l_x(d, x)):
            cp.wait_send()
        for xb in range(NX):
            l_y(d, xb, y).wait_send()
    for k in range(4):
        v_ring(k, z, 0).wait_send()
        if k < 3:
            v_ring(k, z, 1).wait_send()
        for xb in range(NX):
            if k < 3 or xb in UPPER:
                l_ring(k, xb, z, 0).wait_send()
            if k < 3 or xb in LOWER:
                l_ring(k, xb, z, 1).wait_send()
    for zz in range(NZ):
        v_twin(zz, c).wait_send()
        for xb in range(NX):
            l_twin(xb, zz, c).wait_send()
    for j in range(8):
        store(j).wait()


def local(earlier, window_x, off_block, diag_block):
    V, D = pltpu.VMEM, pltpu.SemaphoreType.DMA
    msg = V((CHUNKS, TOK, CW), bf16)
    scratch = [
        V((4 * TOK, COLS), bf16),
        V((TOK, WIN), bf16),
        V((8, TOK, 256), f32),
        V((NX, NZ, 2, ROWS, COLS), bf16),
        V((2, 2, NY, 8, 128), bf16),
        V((2, 128, 128), bf16),
        V((NX, NZ, 2, 2, ROWS, 128), bf16),
        V((NX, NZ, 2, NY, 8, WIN), bf16),
        msg, msg, msg, msg, msg, msg,
        V((4 * TOK, 2 * CW), f32),
        V((4, TOK, CW), f32),
        V((CHUNKS, TOK, CW), f32),
        V((8, 256, 256), bf16),
        V((8, 256, 256), bf16),
        V((8, TOK, 256), f32),
        D((2,)), D((8,)),
        D((2, 4)), D((8,)), D((2, 4)), D((3, 4)), D((4,)), D((CHUNKS,)), D((CHUNKS,)),
        D((3,)), D((3,)), D((3,)), D((3,)), D((3,)), D((3,)), D((2, 4)), D((8,)), D((8,)), D((8,)),
        D((3,)), D((3,)), D((3, 4)), D((3, 4)), D((2, 4, 4)), D((8, 4)), D((8, 4)), D((8, 4)),
        D((3, CHUNKS)), D((3, CHUNKS)),
    ]
    return pl.pallas_call(
        kernel,
        out_shape=jax.ShapeDtypeStruct((TOK, WIN), f32),
        in_specs=[pl.BlockSpec(memory_space=pl.ANY)] * 2 + [pl.BlockSpec(memory_space=V)] * 2,
        out_specs=pl.BlockSpec(memory_space=pl.ANY),
        scratch_shapes=scratch,
        name="whiten",
        compiler_params=pltpu.CompilerParams(
            collective_id=0, has_side_effects=True, vmem_limit_bytes=56 * 2**20
        ),
    )(earlier, window_x, off_block, diag_block)


def solution(mesh):
    return jax.shard_map(
        local,
        mesh=mesh,
        in_specs=(
            P("tok", "feat"),
            P(("tok", "feat"), None),
            P("tok", "feat"),
            P(("tok", "feat"), None),
        ),
        out_specs=P(("tok", "feat"), None),
        check_vma=False,
    )
```

```python
import jax
import jax.numpy as jnp
from jax import lax
from jax.experimental import pallas as pl
from jax.experimental.pallas import tpu as pltpu
from jax.sharding import PartitionSpec as P

f32, bf16 = jnp.float32, jnp.bfloat16
NX, NY, NZ = 4, 4, 8
WIN, COLS, ROWS, TOK = 2048, 1536, 32, 256
CHUNKS, CW = 16, 128
TICKS = 9
FLOOR = 2.0**-10


def split(v):
    high = v.astype(bf16)
    return high, (v - high.astype(f32)).astype(bf16)


def dot(a, b):
    return lax.dot_general(a, b, (((1,), (0,)), ((), ())), preferred_element_type=f32)


def dot_t(a, b):
    return lax.dot_general(a, b, (((1,), (1,)), ((), ())), preferred_element_type=f32)


def encode(v):
    m = jnp.abs(v) + FLOOR
    m2 = m * m
    m4 = m2 * m2
    m12 = m4 * m4 * m4
    return jnp.where(v < 0, -m12, m12).astype(bf16)


def decode(code):
    c = code.astype(f32)
    m = jnp.exp(jnp.log(jnp.abs(c)) * (1.0 / 12.0)) - FLOOR
    return jnp.where(c < 0, -m, m)


def inverse(block):
    n = block.shape[0]
    r = lax.broadcasted_iota(jnp.int32, (n, n), 0)
    c = lax.broadcasted_iota(jnp.int32, (n, n), 1)
    differ = r ^ c
    x = jnp.where(differ == 0, 1.0 / jnp.where(differ == 0, block, 1.0), 0.0)
    s = 1
    while s < n:
        below = jnp.where((differ >= s) & (differ < 2 * s), block, 0.0).astype(bf16)
        xh, xl = split(x)
        th, tl = split(dot(xh, below) + dot(xl, below))
        x = x - (dot(th, xh) + (dot(th, xl) + dot(tl, xh)))
        s *= 2
    return x


FIRST = (0, 3, 10, 21)
PACKED, HALF = 36, 18


def kernel(e_hbm, x_hbm, w_hbm, dg_hbm, out_hbm, e, xw, dg, ov, wb, gb, iv, vb, lx, lp, hs, si, sd, hr, gi, gd, pb, pk, rem, ih, il, acc,
           in_s, out_s, wz_s, wz_r, wx_s, wx_r, wf_s, ws_s, ws_r, gy_s, gy_r, gg_s, gg_r, vx_s, vx_r, vz_s, vz_r, vt_s, vt_r,
           lx_s, lx_r, ly_s, ly_r, lz_s, lz_r, lt_s, lt_r, rs_s, rs_r):
    t, y = lax.axis_index("tok"), lax.axis_index("feat")
    x, z, c = lax.div(t, 16), lax.rem(lax.div(t, 2), 8), lax.rem(t, 2)
    low = lax.rem(z, 2)

    def at(dx=0, dy=0, dz=0, dc=0):
        xx, yy = lax.rem(x + dx + NX, NX), lax.rem(y + dy + NY, NY)
        zz, cc = lax.rem(z + dz + NZ, NZ), lax.rem(c + dc, 2)
        return (xx * 16 + zz * 2 + cc, yy)

    def copy(src, ss, rs, device, dst=None):
        return pltpu.make_async_remote_copy(
            src_ref=src, dst_ref=src if dst is None else dst, send_sem=ss, recv_sem=rs,
            device_id=device, device_id_type=pl.DeviceIdType.MESH)

    load_w = pltpu.make_async_copy(w_hbm, wb.at[x, z, c], in_s.at[0])
    load_dg = pltpu.make_async_copy(dg_hbm, dg, in_s.at[1])
    load_e = pltpu.make_async_copy(e_hbm, e, in_s.at[2])
    load_x = pltpu.make_async_copy(x_hbm, xw, in_s.at[3])
    for load in (load_w, load_dg, load_e, load_x):
        load.start()

    east, west, up, down, twin = at(dx=1), at(dx=-1), at(dz=1), at(dz=-1), at(dc=1)
    mates = [twin, at(dz=1 - 2 * low), at(dz=1 - 2 * low, dc=1)]
    sides = [at(dx=d) for d in (1, 2, 3)]
    others = [at(dy=d) for d in (1, 2, 3)]

    barrier = pltpu.get_barrier_semaphore()
    partners = [up, down, twin, mates[2], *sides, *others]
    for p in partners:
        pl.semaphore_signal(barrier, inc=1, device_id=p, device_id_type=pl.DeviceIdType.MESH)
    pl.semaphore_wait(barrier, len(partners))

    sg = 2 * low - 1

    def pair_of(k):
        off = jnp.where(k == 0, 0, jnp.where(k == 1, sg, jnp.where(k == 2, -sg, 2)))
        return lax.rem(lax.div(z, 2) + off + 4, 4)

    def chunk_of(n):
        side, g = lax.rem(n, 2), lax.div(n, 2)
        own = jnp.logical_or(g == 0, g == 3)
        far = g >= 6
        near_k = jnp.where(g < 3, g - 1, g - 2)
        k = jnp.where(own, jnp.where(g == 0, side, 2 + side), jnp.where(far, n - 12, near_k))
        xs = jnp.where(own, x, jnp.where(far, x + 2, x + 3 + 2 * side))
        return lax.rem(xs, NX), pair_of(k)

    def rows_of(xs, pair, core):
        return wb.at[xs, pl.ds(2 * pair, 2), core]

    def w_ring(k, zsrc, way):
        return copy(wb.at[x, zsrc, c], wz_s.at[way, k], wz_r.at[zsrc], up if way == 0 else down)

    def w_side(k, way):
        return copy(rows_of(x, pair_of(k), c), wx_s.at[way, k], wx_r.at[way, k], east if way == 0 else west)

    def w_near(k, side):
        return copy(rows_of(lax.rem(x + 3 + 2 * side, NX), pair_of(k), c), wf_s.at[k], wx_r.at[side, k], twin)

    def w_on(k):
        side = k % 2
        return copy(rows_of(lax.rem(x + 3 + 2 * side, NX), pair_of(k), c), wf_s.at[k], wx_r.at[2, k], (east, west)[side])

    def w_far(k):
        return copy(rows_of(lax.rem(x + 2, NX), pair_of(k), c), wf_s.at[k], wx_r.at[2, k], twin)

    def w_twin(n, core):
        xs, pair = chunk_of(n)
        return copy(rows_of(xs, pair, core), ws_s.at[n], ws_r.at[n], twin)

    def own_step(k):
        zm, zp = lax.rem(z - (k + 1) + NZ, NZ), lax.rem(z + k + 1, NZ)
        w_ring(0, zm, 0).wait_recv()
        if k < 3:
            w_ring(k + 1, zm, 0).start()
            w_ring(0, zp, 1).wait_recv()
        if k < 2:
            w_ring(k + 1, zp, 1).start()
        w_twin(jnp.int32((0, 1, 6, 7)[k]), c).start()
        w_side(k, 0).start()
        w_side(k, 1).start()

    def near_step(k):
        for side in (0, 1):
            w_near(k, side).wait_recv()
            if side == k % 2:
                w_on(k).start()
            w_twin(jnp.int32((2, 4, 8, 10)[k] + side), c).start()

    def far_step(k):
        w_far(k).wait_recv()
        w_twin(jnp.int32(12 + k), c).start()

    def g_y(d, yy):
        return copy(gb.at[low, c, yy], gy_s.at[d], gy_r.at[d], others[d])

    def g_mate(i, zl, core):
        return copy(gb.at[zl, core], gg_s.at[i], gg_r.at[i], mates[i])

    def v_x(d, xx):
        return copy(vb.at[xx, z, c], vx_s.at[d], vx_r.at[d], sides[d])

    def v_ring(k, zsrc, way):
        return copy(vb.at[:, zsrc, c], vz_s.at[way, k], vz_r.at[zsrc], up if way == 0 else down)

    def v_twin(zsrc, core):
        return copy(vb.at[:, zsrc, core], vt_s.at[zsrc], vt_r.at[zsrc], twin)

    def invert():
        g_mate(0, low, 1 - c).wait_recv()
        g_mate(1, 1 - low, c).wait_recv()
        g_mate(2, 1 - low, 1 - c).wait_recv()
        iv[0], iv[1] = split(inverse(gb[...].reshape(128, 128).astype(f32)))
        mine = pl.ds(pl.multiple_of(32 * (2 * low + c), 32), 32)
        vb[x, z, c, 0] = iv[0, mine]
        vb[x, z, c, 1] = iv[1, mine]
        for d in range(3):
            v_x(d, x).start()

    def v_step(k):
        if k == 0:
            for d in range(3):
                v_x(d, lax.rem(x + 3 - d, NX)).wait_recv()
            v_ring(0, z, 0).start()
            v_ring(0, z, 1).start()
            v_twin(z, c).start()
            return
        zm, zp = lax.rem(z - k + NZ, NZ), lax.rem(z + k, NZ)
        v_ring(0, zm, 0).wait_recv()
        if k < 4:
            v_ring(k, zm, 0).start()
            v_ring(0, zp, 1).wait_recv()
            if k < 3:
                v_ring(k, zp, 1).start()
            v_twin(zp, c).start()
        v_twin(zm, c).start()

    def l_x(d, xx):
        return copy(lx.at[xx], lx_s.at[d], lx_r.at[d], sides[d])

    def l_pack():
        for xb in range(NX):
            for b in range(4 * xb + 3):
                lp[z, c, FIRST[xb] + b, y] = lx[xb, :, 128 * b : 128 * b + 128]

    def l_y(d, yy):
        return copy(lp.at[z, c, :, yy], ly_s.at[d], ly_r.at[d], others[d])

    def l_ring(k, zsrc, way):
        return copy(lp.at[zsrc, c], lz_s.at[way, k], lz_r.at[zsrc, 0], up if way == 0 else down)

    def l_last(zsrc, way):
        half = lp.at[zsrc, c, pl.ds(HALF * way, HALF)]
        return copy(half, lz_s.at[way, 3], lz_r.at[zsrc, way], up if way == 0 else down)

    def l_twin(zsrc, core):
        return copy(lp.at[zsrc, core], lt_s.at[zsrc], lt_r.at[zsrc], twin)

    def l_step(k):
        if k == 0:
            for d in range(3):
                l_y(d, lax.rem(y + 3 - d, NY)).wait_recv()
            l_ring(0, z, 0).start()
            l_ring(0, z, 1).start()
            l_twin(z, c).start()
            return
        zm, zp = lax.rem(z - k + NZ, NZ), lax.rem(z + k, NZ)
        if k == 4:
            l_last(zm, 0).wait_recv()
            l_last(zm, 1).wait_recv()
            l_twin(zm, c).start()
            return
        for zsrc, way in ((zm, 0), (zp, 1)):
            l_ring(0, zsrc, way).wait_recv()
            if k < 3:
                l_ring(k, zsrc, way).start()
            else:
                l_last(zsrc, way).start()
            l_twin(zsrc, c).start()

    def join():
        for zz in range(NZ):
            v_twin(zz, 1 - c).wait_recv()
            l_twin(zz, 1 - c).wait_recv()
        for j in range(8):
            xb, first = j // 2, 4 * (j % 2)
            ah, al = (vb[xb, pl.ds(first, 2), :, h].reshape(128, 128) for h in (0, 1))
            dh, dl = (vb[xb, pl.ds(first + 2, 2), :, h].reshape(128, 128) for h in (0, 1))
            below = lp[pl.ds(first + 2, 2), :, FIRST[xb] + 2 * j].reshape(128, 128)
            th, tl = split(dot(dh, below) + dot(dl, below))
            bh, bl = split(-(dot(th, ah) + (dot(th, al) + dot(tl, ah))))
            zero = jnp.zeros((128, 128), bf16)
            for ref, parts in ((ih, (ah, zero, bh, dh)), (il, (al, zero, bl, dl))):
                ref[j, :128, :128] = parts[0]
                ref[j, :128, 128:] = parts[1]
                ref[j, 128:, :128] = parts[2]
                ref[j, 128:, 128:] = parts[3]

    def sent():
        for k in range(4):
            w_ring(k, z, 0).wait_send()
            if k < 3:
                w_ring(k, z, 1).wait_send()
            w_side(k, 0).wait_send()
            w_side(k, 1).wait_send()
            w_on(k).wait_send()
        for n in range(CHUNKS):
            w_twin(n, c).wait_send()
        for d in range(3):
            for cp in (g_y(d, y), g_mate(d, low, c), v_x(d, x), l_x(d, x), l_y(d, y)):
                cp.wait_send()
        for k in range(4):
            v_ring(k, z, 0).wait_send()
            if k < 3:
                v_ring(k, z, 1).wait_send()
        for k in range(3):
            l_ring(k, z, 0).wait_send()
            l_ring(k, z, 1).wait_send()
        l_last(z, 0).wait_send()
        l_last(z, 1).wait_send()
        for zz in range(NZ):
            v_twin(zz, c).wait_send()
            l_twin(zz, c).wait_send()

    def at_tick(tick, steps):
        for when, do in steps.items():

            @pl.when(tick == when)
            def _(do=do):
                for f, *k in do:
                    f(*k)

    def toward(n):
        return lax.rem(y + 1 + 2 * lax.rem(n, 2), NY)

    def share(kind, n):
        to = toward(n) if kind != 1 else lax.rem(toward(n) + 2, NY)
        src, dst = ((hs, hr), (si, gi), (sd, gd))[kind]
        return copy(src.at[n], rs_s.at[kind, n], rs_r.at[kind, n], (t, to), dst.at[n])

    def rows(n):
        xs, pair = chunk_of(n)
        w_twin(n, 1 - c).wait_recv()
        return wb[xs, pl.ds(2 * pair, 2)].reshape(CW, COLS)

    def hand_out(n, i):
        def part(d):
            return pb[pl.ds(pl.multiple_of(d * TOK, TOK), TOK), pl.ds(CW * i, CW)]

        nd = toward(n)
        hs[n] = encode(part(lax.rem(y + 2, NY)))
        share(0, n).start()
        si[n] = encode(part(lax.rem(nd + 2, NY)))
        share(1, n).start()
        pk[lax.rem(n, 4)] = part(nd)
        xs, pair = chunk_of(n)
        q = 4 * xs + pair
        rem[q] = xw[:, pl.ds(pl.multiple_of(q * CW, CW), CW)].astype(f32) - part(y)

    def pass_on(n):
        share(0, n).wait_recv()
        sd[n] = encode(pk[lax.rem(n, 4)] + decode(hr[n]))
        share(2, n).start()

    def finish(n):
        xs, pair = chunk_of(n)
        q = 4 * xs + pair
        share(1, n).wait_recv()
        share(2, n).wait_recv()
        for kind in range(3):
            share(kind, n).wait_send()
        rem[q] = rem[q] - (decode(gi[n]) + decode(gd[n]))

    def each(tick, do):
        n = jnp.where(tick < 2, tick, 2 * tick - 2)
        do(n)

        @pl.when(tick >= 2)
        def _():
            do(n + 1)

    load_w.wait()
    w_ring(0, z, 0).start()
    w_ring(0, z, 1).start()
    load_dg.wait()
    lx[x] = dg[...]
    gb[low, c, y] = dg[:, pl.ds(pl.multiple_of(lax.div(t, 4) * 128, 128), 128)]
    for d in range(3):
        g_y(d, y).start()
    for d in range(3):
        l_x(d, x).start()
    own_step(0)
    for d in range(3):
        g_y(d, lax.rem(y + 3 - d, NY)).wait_recv()
    for i in range(3):
        g_mate(i, low, c).start()
    for d in range(3):
        l_x(d, lax.rem(x + 3 - d, NX)).wait_recv()
    l_pack()
    for d in range(3):
        l_y(d, y).start()
    load_e.wait()
    load_x.wait()

    @pl.loop(0, TICKS + 2)
    def _(tick):
        @pl.when(tick < 2)
        def _():
            pb[:, pl.ds(0, CW)] = dot_t(e[...], rows(tick))
            hand_out(tick, 0)

        @pl.when(jnp.logical_and(tick >= 2, tick < TICKS))
        def _():
            n = 2 * tick - 2
            pb[...] = dot_t(e[...], jnp.concatenate([rows(n), rows(n + 1)], axis=0))
            hand_out(n, 0)
            hand_out(n + 1, 1)

        at_tick(tick, {
            0: [(own_step, 1)],
            1: [(own_step, 2)],
            2: [(near_step, 1), (own_step, 3)],
            4: [(l_step, 1), (near_step, 2)],
            5: [(near_step, 3)],
            7: [(far_step, 3), (v_step, 2)],
            8: [(v_step, 3)],
            9: [(l_step, 4)],
        })

        @pl.when(jnp.logical_and(tick >= 1, tick <= TICKS))
        def _():
            each(tick - 1, pass_on)

        @pl.when(tick >= 2)
        def _():
            each(tick - 2, finish)

        at_tick(tick, {
            0: [(invert,), (near_step, 0)],
            1: [(l_step, 0)],
            2: [(v_step, 0)],
            4: [(v_step, 1), (far_step, 0), (far_step, 1)],
            5: [(l_step, 2)],
            6: [(far_step, 2)],
            7: [(l_step, 3)],
            8: [(v_step, 4)],
            9: [(sent,), (join,)],
        })

    def store(j):
        return pltpu.make_async_copy(ov.at[j], out_hbm.at[:, pl.ds(256 * j, 256)], out_s.at[j])

    for j in range(8):
        v = jnp.concatenate([rem[2 * j], rem[2 * j + 1]], axis=1)
        if j:
            v = v - acc[j]
        vh, vl = split(v)
        o = dot_t(vh, ih[j]) + (dot_t(vh, il[j]) + dot_t(vl, ih[j]))
        ov[j] = o
        store(j).start()
        oh, ol = split(o)
        for i in range(j + 1, 8):
            at_z, first = pl.ds(4 * (i % 2), 4), FIRST[i // 2] + 2 * j
            block = jnp.concatenate([lp[at_z, :, first + b].reshape(256, 128) for b in (0, 1)], axis=1)
            u = dot_t(oh, block) + dot_t(ol, block)
            acc[i] = u if j == 0 else acc[i] + u

    for j in range(8):
        store(j).wait()


def local(earlier, window_x, off_block, diag_block):
    V, D = pltpu.VMEM, pltpu.SemaphoreType.DMA
    msg = V((CHUNKS, TOK, CW), bf16)
    scratch = [
        V((4 * TOK, COLS), bf16),
        V((TOK, WIN), bf16),
        V((8, WIN), bf16),
        V((8, TOK, 256), f32),
        V((NX, NZ, 2, ROWS, COLS), bf16),
        V((2, 2, NY, 8, 128), bf16),
        V((2, 128, 128), bf16),
        V((NX, NZ, 2, 2, ROWS, 128), bf16),
        V((NX, 8, WIN), bf16),
        V((NZ, 2, PACKED, NY, 8, 128), bf16),
        msg, msg, msg, msg, msg, msg,
        V((4 * TOK, 2 * CW), f32),
        V((4, TOK, CW), f32),
        V((CHUNKS, TOK, CW), f32),
        V((8, 256, 256), bf16),
        V((8, 256, 256), bf16),
        V((8, TOK, 256), f32),
        D((4,)), D((8,)),
        D((2, 4)), D((8,)), D((2, 4)), D((3, 4)), D((4,)), D((CHUNKS,)), D((CHUNKS,)),
        D((3,)), D((3,)), D((3,)), D((3,)), D((3,)), D((3,)), D((2, 4)), D((8,)), D((8,)), D((8,)),
        D((3,)), D((3,)), D((3,)), D((3,)), D((2, 4)), D((8, 2)), D((8,)), D((8,)),
        D((3, CHUNKS)), D((3, CHUNKS)),
    ]
    return pl.pallas_call(
        kernel,
        out_shape=jax.ShapeDtypeStruct((TOK, WIN), f32),
        in_specs=[pl.BlockSpec(memory_space=pl.ANY)] * 4,
        out_specs=pl.BlockSpec(memory_space=pl.ANY),
        scratch_shapes=scratch,
        name="whiten",
        compiler_params=pltpu.CompilerParams(
            collective_id=0, has_side_effects=True, vmem_limit_bytes=56 * 2**20
        ),
    )(earlier, window_x, off_block, diag_block)


def solution(mesh):
    return jax.shard_map(
        local,
        mesh=mesh,
        in_specs=(
            P("tok", "feat"),
            P(("tok", "feat"), None),
            P("tok", "feat"),
            P(("tok", "feat"), None),
        ),
        out_specs=P(("tok", "feat"), None),
        check_vma=False,
    )
```

```python
import jax
import jax.numpy as jnp
from jax import lax
from jax.experimental import pallas as pl
from jax.experimental.pallas import tpu as pltpu
from jax.sharding import PartitionSpec as P

f32, bf16 = jnp.float32, jnp.bfloat16
NX, NY, NZ = 4, 4, 8
WIN, COLS, ROWS, TOK = 2048, 1536, 32, 256
CHUNKS, CW = 16, 128
TICKS, LAG = 9, 2
FLOOR = 2.0**-10


def split(v):
    high = v.astype(bf16)
    return high, (v - high.astype(f32)).astype(bf16)


def dot(a, b):
    return lax.dot_general(a, b, (((1,), (0,)), ((), ())), preferred_element_type=f32)


def dot_t(a, b):
    return lax.dot_general(a, b, (((1,), (1,)), ((), ())), preferred_element_type=f32)


def encode(v):
    m = jnp.abs(v) + FLOOR
    m2 = m * m
    m4 = m2 * m2
    m12 = m4 * m4 * m4
    return jnp.where(v < 0, -m12, m12).astype(bf16)


def decode(code):
    c = code.astype(f32)
    m = jnp.exp(jnp.log(jnp.abs(c)) * (1.0 / 12.0)) - FLOOR
    return jnp.where(c < 0, -m, m)


def inverse(block):
    n = block.shape[0]
    r = lax.broadcasted_iota(jnp.int32, (n, n), 0)
    c = lax.broadcasted_iota(jnp.int32, (n, n), 1)
    differ = r ^ c
    x = jnp.where(differ == 0, 1.0 / jnp.where(differ == 0, block, 1.0), 0.0)
    s = 1
    while s < n:
        below = jnp.where((differ >= s) & (differ < 2 * s), block, 0.0).astype(bf16)
        xh, xl = split(x)
        th, tl = split(dot(xh, below) + dot(xl, below))
        x = x - (dot(th, xh) + (dot(th, xl) + dot(tl, xh)))
        s *= 2
    return x


FIRST = (0, 3, 10, 21)
PACKED, HALF = 36, 18


def kernel(e_hbm, x_hbm, w_hbm, dg_hbm, out_hbm, e, xw, dg, ov, wb, gb, iv, vb, lx, lp, hs, si, sd, hr, gi, gd, pb, pk, rem, ih, il, acc,
           in_s, out_s, wz_s, wz_r, wx_s, wx_r, wf_s, ws_s, ws_r, gy_s, gy_r, gg_s, gg_r, vx_s, vx_r, vz_s, vz_r, vt_s, vt_r,
           lx_s, lx_r, ly_s, ly_r, lz_s, lz_r, lt_s, lt_r, rs_s, rs_r):
    t, y = lax.axis_index("tok"), lax.axis_index("feat")
    x, z, c = lax.div(t, 16), lax.rem(lax.div(t, 2), 8), lax.rem(t, 2)
    low = lax.rem(z, 2)

    def at(dx=0, dy=0, dz=0, dc=0):
        xx, yy = lax.rem(x + dx + NX, NX), lax.rem(y + dy + NY, NY)
        zz, cc = lax.rem(z + dz + NZ, NZ), lax.rem(c + dc, 2)
        return (xx * 16 + zz * 2 + cc, yy)

    def copy(src, ss, rs, device, dst=None):
        return pltpu.make_async_remote_copy(
            src_ref=src, dst_ref=src if dst is None else dst, send_sem=ss, recv_sem=rs,
            device_id=device, device_id_type=pl.DeviceIdType.MESH)

    load_w = pltpu.make_async_copy(w_hbm, wb.at[x, z, c], in_s.at[0])
    load_dg = pltpu.make_async_copy(dg_hbm, dg, in_s.at[1])
    load_e = pltpu.make_async_copy(e_hbm, e, in_s.at[2])
    load_x = pltpu.make_async_copy(x_hbm, xw, in_s.at[3])
    for load in (load_w, load_dg, load_e, load_x):
        load.start()

    east, west, up, down, twin = at(dx=1), at(dx=-1), at(dz=1), at(dz=-1), at(dc=1)
    mates = [twin, at(dz=1 - 2 * low), at(dz=1 - 2 * low, dc=1)]
    sides = [at(dx=d) for d in (1, 2, 3)]
    others = [at(dy=d) for d in (1, 2, 3)]

    barrier = pltpu.get_barrier_semaphore()
    partners = [up, down, twin, mates[2], *sides, *others]
    for p in partners:
        pl.semaphore_signal(barrier, inc=1, device_id=p, device_id_type=pl.DeviceIdType.MESH)
    pl.semaphore_wait(barrier, len(partners))

    sg = 2 * low - 1

    def pair_of(k):
        off = jnp.where(k == 0, 0, jnp.where(k == 1, sg, jnp.where(k == 2, -sg, 2)))
        return lax.rem(lax.div(z, 2) + off + 4, 4)

    def chunk_of(n):
        side, g = lax.rem(n, 2), lax.div(n, 2)
        own = jnp.logical_or(g == 0, g == 3)
        far = g >= 6
        near_k = jnp.where(g < 3, g - 1, g - 2)
        k = jnp.where(own, jnp.where(g == 0, side, 2 + side), jnp.where(far, n - 12, near_k))
        xs = jnp.where(own, x, jnp.where(far, x + 2, x + 3 + 2 * side))
        return lax.rem(xs, NX), pair_of(k)

    def rows_of(xs, pair, core):
        return wb.at[xs, pl.ds(2 * pair, 2), core]

    def w_ring(k, zsrc, way):
        return copy(wb.at[x, zsrc, c], wz_s.at[way, k], wz_r.at[zsrc], up if way == 0 else down)

    def w_side(k, way):
        return copy(rows_of(x, pair_of(k), c), wx_s.at[way, k], wx_r.at[way, k], east if way == 0 else west)

    def w_near(k, side):
        return copy(rows_of(lax.rem(x + 3 + 2 * side, NX), pair_of(k), c), wf_s.at[k], wx_r.at[side, k], twin)

    def w_on(k):
        side = k % 2
        return copy(rows_of(lax.rem(x + 3 + 2 * side, NX), pair_of(k), c), wf_s.at[k], wx_r.at[2, k], (east, west)[side])

    def w_far(k):
        return copy(rows_of(lax.rem(x + 2, NX), pair_of(k), c), wf_s.at[k], wx_r.at[2, k], twin)

    def w_twin(n, core):
        xs, pair = chunk_of(n)
        return copy(rows_of(xs, pair, core), ws_s.at[n], ws_r.at[n], twin)

    def own_step(k):
        zm, zp = lax.rem(z - (k + 1) + NZ, NZ), lax.rem(z + k + 1, NZ)
        w_ring(0, zm, 0).wait_recv()
        if k < 3:
            w_ring(k + 1, zm, 0).start()
            w_ring(0, zp, 1).wait_recv()
        if k < 2:
            w_ring(k + 1, zp, 1).start()
        w_twin(jnp.int32((0, 1, 6, 7)[k]), c).start()
        w_side(k, 0).start()
        w_side(k, 1).start()

    def near_step(k):
        for side in (0, 1):
            w_near(k, side).wait_recv()
            if side == k % 2:
                w_on(k).start()
            w_twin(jnp.int32((2, 4, 8, 10)[k] + side), c).start()

    def far_step(k):
        w_far(k).wait_recv()
        w_twin(jnp.int32(12 + k), c).start()

    def g_y(d, yy):
        return copy(gb.at[low, c, yy], gy_s.at[d], gy_r.at[d], others[d])

    def g_mate(i, zl, core):
        return copy(gb.at[zl, core], gg_s.at[i], gg_r.at[i], mates[i])

    def v_x(d, xx):
        return copy(vb.at[xx, z, c], vx_s.at[d], vx_r.at[d], sides[d])

    def v_ring(k, zsrc, way):
        return copy(vb.at[:, zsrc, c], vz_s.at[way, k], vz_r.at[zsrc], up if way == 0 else down)

    def v_twin(zsrc, core):
        return copy(vb.at[:, zsrc, core], vt_s.at[zsrc], vt_r.at[zsrc], twin)

    def invert():
        g_mate(0, low, 1 - c).wait_recv()
        g_mate(1, 1 - low, c).wait_recv()
        g_mate(2, 1 - low, 1 - c).wait_recv()
        iv[0], iv[1] = split(inverse(gb[...].reshape(128, 128).astype(f32)))
        mine = pl.ds(pl.multiple_of(32 * (2 * low + c), 32), 32)
        vb[x, z, c, 0] = iv[0, mine]
        vb[x, z, c, 1] = iv[1, mine]
        for d in range(3):
            v_x(d, x).start()

    def v_step(k):
        if k == 0:
            for d in range(3):
                v_x(d, lax.rem(x + 3 - d, NX)).wait_recv()
            v_ring(0, z, 0).start()
            v_ring(0, z, 1).start()
            v_twin(z, c).start()
            return
        zm, zp = lax.rem(z - k + NZ, NZ), lax.rem(z + k, NZ)
        v_ring(0, zm, 0).wait_recv()
        if k < 4:
            v_ring(k, zm, 0).start()
            v_ring(0, zp, 1).wait_recv()
            if k < 3:
                v_ring(k, zp, 1).start()
            v_twin(zp, c).start()
        v_twin(zm, c).start()

    def l_x(d, xx):
        return copy(lx.at[xx], lx_s.at[d], lx_r.at[d], sides[d])

    def l_pack():
        for xb in range(NX):
            for b in range(4 * xb + 3):
                lp[z, c, FIRST[xb] + b, y] = lx[xb, :, 128 * b : 128 * b + 128]

    def l_y(d, yy):
        return copy(lp.at[z, c, :, yy], ly_s.at[d], ly_r.at[d], others[d])

    def l_ring(k, zsrc, way):
        return copy(lp.at[zsrc, c], lz_s.at[way, k], lz_r.at[zsrc, 0], up if way == 0 else down)

    def l_last(zsrc, way):
        half = lp.at[zsrc, c, pl.ds(HALF * way, HALF)]
        return copy(half, lz_s.at[way, 3], lz_r.at[zsrc, way], up if way == 0 else down)

    def l_twin(zsrc, core):
        return copy(lp.at[zsrc, core], lt_s.at[zsrc], lt_r.at[zsrc], twin)

    def l_step(k):
        if k == 0:
            for d in range(3):
                l_y(d, lax.rem(y + 3 - d, NY)).wait_recv()
            l_ring(0, z, 0).start()
            l_ring(0, z, 1).start()
            l_twin(z, c).start()
            return
        zm, zp = lax.rem(z - k + NZ, NZ), lax.rem(z + k, NZ)
        if k == 4:
            l_last(zm, 0).wait_recv()
            l_last(zm, 1).wait_recv()
            l_twin(zm, c).start()
            return
        for zsrc, way in ((zm, 0), (zp, 1)):
            l_ring(0, zsrc, way).wait_recv()
            if k < 3:
                l_ring(k, zsrc, way).start()
            else:
                l_last(zsrc, way).start()
            l_twin(zsrc, c).start()

    half = lax.div(z, 4)

    def join(far):
        side = 1 - half if far else half
        for i in range(4):
            v_twin(4 * side + i, 1 - c).wait_recv()
            l_twin(4 * side + i, 1 - c).wait_recv()
        for xb in range(NX):
            j = 2 * xb + side
            a, d = pl.ds(4 * side, 2), pl.ds(4 * side + 2, 2)
            ah, al = (vb[xb, a, :, h].reshape(128, 128) for h in (0, 1))
            dh, dl = (vb[xb, d, :, h].reshape(128, 128) for h in (0, 1))
            below = lp[d, :, FIRST[xb] + 2 * j].reshape(128, 128)
            th, tl = split(dot(dh, below) + dot(dl, below))
            bh, bl = split(-(dot(th, ah) + (dot(th, al) + dot(tl, ah))))
            zero = jnp.zeros((128, 128), bf16)
            for ref, parts in ((ih, (ah, zero, bh, dh)), (il, (al, zero, bl, dl))):
                ref[j, :128, :128] = parts[0]
                ref[j, :128, 128:] = parts[1]
                ref[j, 128:, :128] = parts[2]
                ref[j, 128:, 128:] = parts[3]

    def sent():
        for k in range(4):
            w_ring(k, z, 0).wait_send()
            if k < 3:
                w_ring(k, z, 1).wait_send()
            w_side(k, 0).wait_send()
            w_side(k, 1).wait_send()
            w_on(k).wait_send()
        for n in range(CHUNKS):
            w_twin(n, c).wait_send()
        for d in range(3):
            for cp in (g_y(d, y), g_mate(d, low, c), v_x(d, x), l_x(d, x), l_y(d, y)):
                cp.wait_send()
        for k in range(4):
            v_ring(k, z, 0).wait_send()
            if k < 3:
                v_ring(k, z, 1).wait_send()
        for k in range(3):
            l_ring(k, z, 0).wait_send()
            l_ring(k, z, 1).wait_send()
        l_last(z, 0).wait_send()
        l_last(z, 1).wait_send()
        for zz in range(NZ):
            v_twin(zz, c).wait_send()
            l_twin(zz, c).wait_send()

    def at_tick(tick, steps):
        for when, do in steps.items():

            @pl.when(tick == when)
            def _(do=do):
                for f, *k in do:
                    f(*k)

    def toward(n):
        return lax.rem(y + 1 + 2 * lax.rem(n, 2), NY)

    def share(kind, n):
        to = toward(n) if kind != 1 else lax.rem(toward(n) + 2, NY)
        src, dst = ((hs, hr), (si, gi), (sd, gd))[kind]
        return copy(src.at[n], rs_s.at[kind, n], rs_r.at[kind, n], (t, to), dst.at[n])

    def rows(n):
        xs, pair = chunk_of(n)
        w_twin(n, 1 - c).wait_recv()
        return wb[xs, pl.ds(2 * pair, 2)].reshape(CW, COLS)

    def hand_out(n, i):
        def part(d):
            return pb[pl.ds(pl.multiple_of(d * TOK, TOK), TOK), pl.ds(CW * i, CW)]

        nd = toward(n)
        hs[n] = encode(part(lax.rem(y + 2, NY)))
        share(0, n).start()
        si[n] = encode(part(lax.rem(nd + 2, NY)))
        share(1, n).start()
        pk[lax.rem(n, 4)] = part(nd)
        xs, pair = chunk_of(n)
        q = 4 * xs + pair
        rem[q] = xw[:, pl.ds(pl.multiple_of(q * CW, CW), CW)].astype(f32) - part(y)

    def pass_on(n):
        share(0, n).wait_recv()
        sd[n] = encode(pk[lax.rem(n, 4)] + decode(hr[n]))
        share(2, n).start()

    def finish(n):
        xs, pair = chunk_of(n)
        q = 4 * xs + pair
        share(1, n).wait_recv()
        share(2, n).wait_recv()
        for kind in range(3):
            share(kind, n).wait_send()
        rem[q] = rem[q] - (decode(gi[n]) + decode(gd[n]))

    def each(tick, do):
        n = jnp.where(tick < 2, tick, 2 * tick - 2)
        do(n)

        @pl.when(tick >= 2)
        def _():
            do(n + 1)

    load_w.wait()
    w_ring(0, z, 0).start()
    w_ring(0, z, 1).start()
    load_dg.wait()
    lx[x] = dg[...]
    gb[low, c, y] = dg[:, pl.ds(pl.multiple_of(lax.div(t, 4) * 128, 128), 128)]
    for d in range(3):
        g_y(d, y).start()
    for d in range(3):
        l_x(d, x).start()
    own_step(0)
    for d in range(3):
        g_y(d, lax.rem(y + 3 - d, NY)).wait_recv()
    for i in range(3):
        g_mate(i, low, c).start()
    for d in range(3):
        l_x(d, lax.rem(x + 3 - d, NX)).wait_recv()
    l_pack()
    for d in range(3):
        l_y(d, y).start()
    load_e.wait()
    load_x.wait()

    @pl.loop(0, TICKS + LAG)
    def _(tick):
        @pl.when(tick < 2)
        def _():
            pb[:, pl.ds(0, CW)] = dot_t(e[...], rows(tick))
            hand_out(tick, 0)

        @pl.when(jnp.logical_and(tick >= 2, tick < TICKS))
        def _():
            n = 2 * tick - 2
            pb[...] = dot_t(e[...], jnp.concatenate([rows(n), rows(n + 1)], axis=0))
            hand_out(n, 0)
            hand_out(n + 1, 1)

        at_tick(tick, {
            0: [(own_step, 1)],
            1: [(own_step, 2), (l_step, 0)],
            2: [(near_step, 1)],
            4: [(l_step, 1), (far_step, 0), (near_step, 2), (v_step, 1)],
            5: [(near_step, 3)],
            6: [(far_step, 2)],
            7: [(l_step, 3)],
            8: [(v_step, 3)],
            9: [(v_step, 4)],
        })

        @pl.when(jnp.logical_and(tick >= 1, tick <= TICKS))
        def _():
            each(tick - 1, pass_on)

        @pl.when(tick >= LAG)
        def _():
            each(tick - LAG, finish)

        at_tick(tick, {
            0: [(invert,), (near_step, 0)],
            2: [(v_step, 0), (own_step, 3)],
            4: [(far_step, 1)],
            5: [(l_step, 2)],
            6: [(far_step, 3), (v_step, 2)],
            8: [(l_step, 4), (join, False)],
            9: [(join, True), (sent,)],
        })

    def store(j):
        return pltpu.make_async_copy(ov.at[j], out_hbm.at[:, pl.ds(256 * j, 256)], out_s.at[j])

    for j in range(8):
        v = jnp.concatenate([rem[2 * j], rem[2 * j + 1]], axis=1)
        if j:
            v = v - acc[j]
        vh, vl = split(v)
        o = dot_t(vh, ih[j]) + (dot_t(vh, il[j]) + dot_t(vl, ih[j]))
        ov[j] = o
        store(j).start()
        oh, ol = split(o)
        for i in range(j + 1, 8):
            at_z, first = pl.ds(4 * (i % 2), 4), FIRST[i // 2] + 2 * j
            block = jnp.concatenate([lp[at_z, :, first + b].reshape(256, 128) for b in (0, 1)], axis=1)
            u = dot_t(oh, block) + dot_t(ol, block)
            acc[i] = u if j == 0 else acc[i] + u

    for j in range(8):
        store(j).wait()


def local(earlier, window_x, off_block, diag_block):
    V, D = pltpu.VMEM, pltpu.SemaphoreType.DMA
    msg = V((CHUNKS, TOK, CW), bf16)
    scratch = [
        V((4 * TOK, COLS), bf16),
        V((TOK, WIN), bf16),
        V((8, WIN), bf16),
        V((8, TOK, 256), f32),
        V((NX, NZ, 2, ROWS, COLS), bf16),
        V((2, 2, NY, 8, 128), bf16),
        V((2, 128, 128), bf16),
        V((NX, NZ, 2, 2, ROWS, 128), bf16),
        V((NX, 8, WIN), bf16),
        V((NZ, 2, PACKED, NY, 8, 128), bf16),
        msg, msg, msg, msg, msg, msg,
        V((4 * TOK, 2 * CW), f32),
        V((4, TOK, CW), f32),
        V((CHUNKS, TOK, CW), f32),
        V((8, 256, 256), bf16),
        V((8, 256, 256), bf16),
        V((8, TOK, 256), f32),
        D((4,)), D((8,)),
        D((2, 4)), D((8,)), D((2, 4)), D((3, 4)), D((4,)), D((CHUNKS,)), D((CHUNKS,)),
        D((3,)), D((3,)), D((3,)), D((3,)), D((3,)), D((3,)), D((2, 4)), D((8,)), D((8,)), D((8,)),
        D((3,)), D((3,)), D((3,)), D((3,)), D((2, 4)), D((8, 2)), D((8,)), D((8,)),
        D((3, CHUNKS)), D((3, CHUNKS)),
    ]
    return pl.pallas_call(
        kernel,
        out_shape=jax.ShapeDtypeStruct((TOK, WIN), f32),
        in_specs=[pl.BlockSpec(memory_space=pl.ANY)] * 4,
        out_specs=pl.BlockSpec(memory_space=pl.ANY),
        scratch_shapes=scratch,
        name="whiten",
        compiler_params=pltpu.CompilerParams(
            collective_id=0, has_side_effects=True, vmem_limit_bytes=56 * 2**20
        ),
    )(earlier, window_x, off_block, diag_block)


def solution(mesh):
    return jax.shard_map(
        local,
        mesh=mesh,
        in_specs=(
            P("tok", "feat"),
            P(("tok", "feat"), None),
            P("tok", "feat"),
            P(("tok", "feat"), None),
        ),
        out_specs=P(("tok", "feat"), None),
        check_vma=False,
    )
```

```python
import jax
import jax.numpy as jnp
from jax import lax
from jax.experimental import pallas as pl
from jax.experimental.pallas import tpu as pltpu
from jax.sharding import PartitionSpec as P

f32, bf16 = jnp.float32, jnp.bfloat16
NX, NY, NZ = 4, 4, 8
WIN, COLS, ROWS, TOK = 2048, 1536, 32, 256
CHUNKS, CW = 16, 128
TICKS, LAG = 9, 2
FLOOR = 2.0**-10


def split(v):
    high = v.astype(bf16)
    return high, (v - high.astype(f32)).astype(bf16)


def dot(a, b):
    return lax.dot_general(a, b, (((1,), (0,)), ((), ())), preferred_element_type=f32)


def dot_t(a, b):
    return lax.dot_general(a, b, (((1,), (1,)), ((), ())), preferred_element_type=f32)


def encode(v):
    m = jnp.abs(v) + FLOOR
    m2 = m * m
    m4 = m2 * m2
    m12 = m4 * m4 * m4
    return jnp.where(v < 0, -m12, m12).astype(bf16)


def decode(code):
    c = code.astype(f32)
    m = jnp.exp(jnp.log(jnp.abs(c)) * (1.0 / 12.0)) - FLOOR
    return jnp.where(c < 0, -m, m)


def inverse(block):
    n = block.shape[0]
    r = lax.broadcasted_iota(jnp.int32, (n, n), 0)
    c = lax.broadcasted_iota(jnp.int32, (n, n), 1)
    differ = r ^ c
    x = jnp.where(differ == 0, 1.0 / jnp.where(differ == 0, block, 1.0), 0.0)
    s = 1
    while s < n:
        below = jnp.where((differ >= s) & (differ < 2 * s), block, 0.0).astype(bf16)
        xh, xl = split(x)
        th, tl = split(dot(xh, below) + dot(xl, below))
        x = x - (dot(th, xh) + (dot(th, xl) + dot(tl, xh)))
        s *= 2
    return x


FIRST = (0, 3, 10, 21)
PACKED, HALF = 36, 18


def kernel(e_hbm, x_hbm, w_hbm, dg_hbm, out_hbm, e, xw, dg, ov, wb, gb, iv, vb, lx, lp, hs, si, sd, hr, gi, gd, pb, pk, rem, ih, il, acc,
           in_s, out_s, wz_s, wz_r, wx_s, wx_r, wf_s, ws_s, ws_r, gy_s, gy_r, gg_s, gg_r, vx_s, vx_r, vz_s, vz_r, vt_s, vt_r,
           lx_s, lx_r, ly_s, ly_r, lz_s, lz_r, lt_s, lt_r, rs_s, rs_r):
    t, y = lax.axis_index("tok"), lax.axis_index("feat")
    x, z, c = lax.div(t, 16), lax.rem(lax.div(t, 2), 8), lax.rem(t, 2)
    low = lax.rem(z, 2)

    def at(dx=0, dy=0, dz=0, dc=0):
        xx, yy = lax.rem(x + dx + NX, NX), lax.rem(y + dy + NY, NY)
        zz, cc = lax.rem(z + dz + NZ, NZ), lax.rem(c + dc, 2)
        return (xx * 16 + zz * 2 + cc, yy)

    def copy(src, ss, rs, device, dst=None):
        return pltpu.make_async_remote_copy(
            src_ref=src, dst_ref=src if dst is None else dst, send_sem=ss, recv_sem=rs,
            device_id=device, device_id_type=pl.DeviceIdType.MESH)

    load_w = pltpu.make_async_copy(w_hbm, wb.at[x, z, c], in_s.at[0])
    load_dg = pltpu.make_async_copy(dg_hbm, dg, in_s.at[1])
    load_e = pltpu.make_async_copy(e_hbm, e, in_s.at[2])
    load_x = pltpu.make_async_copy(x_hbm, xw, in_s.at[3])
    for load in (load_w, load_dg, load_e, load_x):
        load.start()

    east, west, up, down, twin = at(dx=1), at(dx=-1), at(dz=1), at(dz=-1), at(dc=1)
    mates = [twin, at(dz=1 - 2 * low), at(dz=1 - 2 * low, dc=1)]
    sides = [at(dx=d) for d in (1, 2, 3)]
    others = [at(dy=d) for d in (1, 2, 3)]

    barrier = pltpu.get_barrier_semaphore()
    partners = [up, down, twin, mates[2], *sides, *others]
    for p in partners:
        pl.semaphore_signal(barrier, inc=1, device_id=p, device_id_type=pl.DeviceIdType.MESH)
    pl.semaphore_wait(barrier, len(partners))

    sg = 2 * low - 1

    def pair_of(k):
        off = jnp.where(k == 0, 0, jnp.where(k == 1, sg, jnp.where(k == 2, -sg, 2)))
        return lax.rem(lax.div(z, 2) + off + 4, 4)

    def chunk_of(n):
        side, g = lax.rem(n, 2), lax.div(n, 2)
        own = jnp.logical_or(g == 0, g == 3)
        far = g >= 6
        near_k = jnp.where(g < 3, g - 1, g - 2)
        k = jnp.where(own, jnp.where(g == 0, side, 2 + side), jnp.where(far, n - 12, near_k))
        xs = jnp.where(own, x, jnp.where(far, x + 2, x + 3 + 2 * side))
        return lax.rem(xs, NX), pair_of(k)

    def rows_of(xs, pair, core):
        return wb.at[xs, pl.ds(2 * pair, 2), core]

    def w_ring(k, zsrc, way):
        return copy(wb.at[x, zsrc, c], wz_s.at[way, k], wz_r.at[zsrc], up if way == 0 else down)

    def w_side(k, way):
        return copy(rows_of(x, pair_of(k), c), wx_s.at[way, k], wx_r.at[way, k], east if way == 0 else west)

    def w_near(k, side):
        return copy(rows_of(lax.rem(x + 3 + 2 * side, NX), pair_of(k), c), wf_s.at[k], wx_r.at[side, k], twin)

    def w_on(k):
        side = k % 2
        return copy(rows_of(lax.rem(x + 3 + 2 * side, NX), pair_of(k), c), wf_s.at[k], wx_r.at[2, k], (east, west)[side])

    def w_far(k):
        return copy(rows_of(lax.rem(x + 2, NX), pair_of(k), c), wf_s.at[k], wx_r.at[2, k], twin)

    def w_twin(n, core):
        xs, pair = chunk_of(n)
        return copy(rows_of(xs, pair, core), ws_s.at[n], ws_r.at[n], twin)

    def own_step(k):
        zm, zp = lax.rem(z - (k + 1) + NZ, NZ), lax.rem(z + k + 1, NZ)
        w_ring(0, zm, 0).wait_recv()
        if k < 3:
            w_ring(k + 1, zm, 0).start()
            w_ring(0, zp, 1).wait_recv()
        if k < 2:
            w_ring(k + 1, zp, 1).start()
        w_twin(jnp.int32((0, 1, 6, 7)[k]), c).start()
        w_side(k, 0).start()
        w_side(k, 1).start()

    def near_step(k):
        for side in (0, 1):
            w_near(k, side).wait_recv()
            if side == k % 2:
                w_on(k).start()
            w_twin(jnp.int32((2, 4, 8, 10)[k] + side), c).start()

    def far_step(k):
        w_far(k).wait_recv()
        w_twin(jnp.int32(12 + k), c).start()

    def g_y(d, yy):
        return copy(gb.at[low, c, yy], gy_s.at[d], gy_r.at[d], others[d])

    def g_mate(i, zl, core):
        return copy(gb.at[zl, core], gg_s.at[i], gg_r.at[i], mates[i])

    def v_x(d, xx):
        return copy(vb.at[xx, z, c], vx_s.at[d], vx_r.at[d], sides[d])

    def v_ring(k, zsrc, way):
        return copy(vb.at[:, zsrc, c], vz_s.at[way, k], vz_r.at[zsrc], up if way == 0 else down)

    def v_twin(zsrc, core):
        return copy(vb.at[:, zsrc, core], vt_s.at[zsrc], vt_r.at[zsrc], twin)

    def invert():
        g_mate(0, low, 1 - c).wait_recv()
        g_mate(1, 1 - low, c).wait_recv()
        g_mate(2, 1 - low, 1 - c).wait_recv()
        iv[0], iv[1] = split(inverse(gb[...].reshape(128, 128).astype(f32)))
        mine = pl.ds(pl.multiple_of(32 * (2 * low + c), 32), 32)
        vb[x, z, c, 0] = iv[0, mine]
        vb[x, z, c, 1] = iv[1, mine]
        for d in range(3):
            v_x(d, x).start()

    def v_step(k):
        if k == 0:
            for d in range(3):
                v_x(d, lax.rem(x + 3 - d, NX)).wait_recv()
            v_ring(0, z, 0).start()
            v_ring(0, z, 1).start()
            v_twin(z, c).start()
            return
        zm, zp = lax.rem(z - k + NZ, NZ), lax.rem(z + k, NZ)
        v_ring(0, zm, 0).wait_recv()
        if k < 4:
            v_ring(k, zm, 0).start()
            v_ring(0, zp, 1).wait_recv()
            if k < 3:
                v_ring(k, zp, 1).start()
            v_twin(zp, c).start()
        v_twin(zm, c).start()

    def l_x(d, xx):
        return copy(lx.at[xx], lx_s.at[d], lx_r.at[d], sides[d])

    def l_pack():
        for xb in range(NX):
            for b in range(4 * xb + 3):
                lp[z, c, FIRST[xb] + b, y] = lx[xb, :, 128 * b : 128 * b + 128]

    def l_y(d, yy):
        return copy(lp.at[z, c, :, yy], ly_s.at[d], ly_r.at[d], others[d])

    def l_ring(k, zsrc, way):
        return copy(lp.at[zsrc, c], lz_s.at[way, k], lz_r.at[zsrc, 0], up if way == 0 else down)

    def l_last(zsrc, way):
        half = lp.at[zsrc, c, pl.ds(HALF * way, HALF)]
        return copy(half, lz_s.at[way, 3], lz_r.at[zsrc, way], up if way == 0 else down)

    def l_twin(zsrc, core):
        return copy(lp.at[zsrc, core], lt_s.at[zsrc], lt_r.at[zsrc], twin)

    def l_step(k):
        if k == 0:
            for d in range(3):
                l_y(d, lax.rem(y + 3 - d, NY)).wait_recv()
            l_ring(0, z, 0).start()
            l_ring(0, z, 1).start()
            l_twin(z, c).start()
            return
        zm, zp = lax.rem(z - k + NZ, NZ), lax.rem(z + k, NZ)
        if k == 4:
            l_last(zm, 0).wait_recv()
            l_last(zm, 1).wait_recv()
            l_twin(zm, c).start()
            return
        for zsrc, way in ((zm, 0), (zp, 1)):
            l_ring(0, zsrc, way).wait_recv()
            if k < 3:
                l_ring(k, zsrc, way).start()
            else:
                l_last(zsrc, way).start()
            l_twin(zsrc, c).start()

    half = lax.div(z, 4)

    def join(far):
        side = 1 - half if far else half
        for i in range(4):
            v_twin(4 * side + i, 1 - c).wait_recv()
            l_twin(4 * side + i, 1 - c).wait_recv()
        for xb in range(NX):
            j = 2 * xb + side
            a, d = pl.ds(4 * side, 2), pl.ds(4 * side + 2, 2)
            ah, al = (vb[xb, a, :, h].reshape(128, 128) for h in (0, 1))
            dh, dl = (vb[xb, d, :, h].reshape(128, 128) for h in (0, 1))
            below = lp[d, :, FIRST[xb] + 2 * j].reshape(128, 128)
            th, tl = split(dot(dh, below) + dot(dl, below))
            bh, bl = split(-(dot(th, ah) + (dot(th, al) + dot(tl, ah))))
            zero = jnp.zeros((128, 128), bf16)
            for ref, parts in ((ih, (ah, zero, bh, dh)), (il, (al, zero, bl, dl))):
                ref[j, :128, :128] = parts[0]
                ref[j, :128, 128:] = parts[1]
                ref[j, 128:, :128] = parts[2]
                ref[j, 128:, 128:] = parts[3]

    def sent():
        for k in range(4):
            w_ring(k, z, 0).wait_send()
            if k < 3:
                w_ring(k, z, 1).wait_send()
            w_side(k, 0).wait_send()
            w_side(k, 1).wait_send()
            w_on(k).wait_send()
        for n in range(CHUNKS):
            w_twin(n, c).wait_send()
        for d in range(3):
            for cp in (g_y(d, y), g_mate(d, low, c), v_x(d, x), l_x(d, x), l_y(d, y)):
                cp.wait_send()
        for k in range(4):
            v_ring(k, z, 0).wait_send()
            if k < 3:
                v_ring(k, z, 1).wait_send()
        for k in range(3):
            l_ring(k, z, 0).wait_send()
            l_ring(k, z, 1).wait_send()
        l_last(z, 0).wait_send()
        l_last(z, 1).wait_send()
        for zz in range(NZ):
            v_twin(zz, c).wait_send()
            l_twin(zz, c).wait_send()

    def at_tick(tick, steps):
        for when, do in steps.items():

            @pl.when(tick == when)
            def _(do=do):
                for f, *k in do:
                    f(*k)

    def toward(n):
        return lax.rem(y + 1 + 2 * lax.rem(n, 2), NY)

    def share(kind, n):
        to = toward(n) if kind != 1 else lax.rem(toward(n) + 2, NY)
        src, dst = ((hs, hr), (si, gi), (sd, gd))[kind]
        return copy(src.at[n], rs_s.at[kind, n], rs_r.at[kind, n], (t, to), dst.at[n])

    def rows(n):
        xs, pair = chunk_of(n)
        w_twin(n, 1 - c).wait_recv()
        return wb[xs, pl.ds(2 * pair, 2)].reshape(CW, COLS)

    def hand_out(n, i):
        def part(d):
            return pb[pl.ds(pl.multiple_of(d * TOK, TOK), TOK), pl.ds(CW * i, CW)]

        nd = toward(n)
        hs[n] = encode(part(lax.rem(y + 2, NY)))
        share(0, n).start()
        si[n] = encode(part(lax.rem(nd + 2, NY)))
        share(1, n).start()
        pk[lax.rem(n, 4)] = part(nd)
        xs, pair = chunk_of(n)
        q = 4 * xs + pair
        rem[q] = xw[:, pl.ds(pl.multiple_of(q * CW, CW), CW)].astype(f32) - part(y)

    def pass_on(n):
        share(0, n).wait_recv()
        sd[n] = encode(pk[lax.rem(n, 4)] + decode(hr[n]))
        share(2, n).start()

    def finish(n):
        xs, pair = chunk_of(n)
        q = 4 * xs + pair
        share(1, n).wait_recv()
        share(2, n).wait_recv()
        for kind in range(3):
            share(kind, n).wait_send()
        rem[q] = rem[q] - (decode(gi[n]) + decode(gd[n]))

    def each(tick, do):
        n = jnp.where(tick < 2, tick, 2 * tick - 2)
        do(n)

        @pl.when(tick >= 2)
        def _():
            do(n + 1)

    load_w.wait()
    w_ring(0, z, 0).start()
    w_ring(0, z, 1).start()
    load_dg.wait()
    lx[x] = dg[...]
    gb[low, c, y] = dg[:, pl.ds(pl.multiple_of(lax.div(t, 4) * 128, 128), 128)]
    for d in range(3):
        g_y(d, y).start()
    for d in range(3):
        l_x(d, x).start()
    own_step(0)
    for d in range(3):
        g_y(d, lax.rem(y + 3 - d, NY)).wait_recv()
    for i in range(3):
        g_mate(i, low, c).start()
    for d in range(3):
        l_x(d, lax.rem(x + 3 - d, NX)).wait_recv()
    l_pack()
    for d in range(3):
        l_y(d, y).start()
    load_e.wait()
    load_x.wait()

    @pl.loop(0, TICKS + LAG)
    def _(tick):
        @pl.when(tick < 2)
        def _():
            pb[:, pl.ds(0, CW)] = dot_t(e[...], rows(tick))
            hand_out(tick, 0)

        @pl.when(jnp.logical_and(tick >= 2, tick < TICKS))
        def _():
            n = 2 * tick - 2
            pb[...] = dot_t(e[...], jnp.concatenate([rows(n), rows(n + 1)], axis=0))
            hand_out(n, 0)
            hand_out(n + 1, 1)

        at_tick(tick, {
            0: [(own_step, 1)],
            1: [(own_step, 2), (l_step, 0)],
            2: [(near_step, 1)],
            4: [(l_step, 1), (far_step, 0), (near_step, 2), (v_step, 1)],
            5: [(near_step, 3)],
            6: [(far_step, 2)],
            7: [(l_step, 3)],
            8: [(v_step, 3)],
            9: [(v_step, 4)],
        })

        @pl.when(jnp.logical_and(tick >= 1, tick <= TICKS))
        def _():
            each(tick - 1, pass_on)

        @pl.when(tick >= LAG)
        def _():
            each(tick - LAG, finish)

        at_tick(tick, {
            0: [(invert,), (near_step, 0)],
            2: [(v_step, 0), (own_step, 3)],
            4: [(far_step, 1)],
            5: [(l_step, 2)],
            6: [(far_step, 3), (v_step, 2)],
            8: [(l_step, 4), (join, False)],
            9: [(join, True)],
        })

    def store(j):
        return pltpu.make_async_copy(ov.at[j], out_hbm.at[:, pl.ds(256 * j, 256)], out_s.at[j])

    for j in range(8):
        v = jnp.concatenate([rem[2 * j], rem[2 * j + 1]], axis=1)
        if j:
            v = v - acc[j]
        vh, vl = split(v)
        o = dot_t(vh, ih[j]) + (dot_t(vh, il[j]) + dot_t(vl, ih[j]))
        ov[j] = o
        store(j).start()
        oh, ol = split(o)
        for i in range(j + 1, 8):
            at_z, first = pl.ds(4 * (i % 2), 4), FIRST[i // 2] + 2 * j
            block = jnp.concatenate([lp[at_z, :, first + b].reshape(256, 128) for b in (0, 1)], axis=1)
            u = dot_t(oh, block) + dot_t(ol, block)
            acc[i] = u if j == 0 else acc[i] + u

    sent()
    for j in range(8):
        store(j).wait()


def local(earlier, window_x, off_block, diag_block):
    V, D = pltpu.VMEM, pltpu.SemaphoreType.DMA
    msg = V((CHUNKS, TOK, CW), bf16)
    scratch = [
        V((4 * TOK, COLS), bf16),
        V((TOK, WIN), bf16),
        V((8, WIN), bf16),
        V((8, TOK, 256), f32),
        V((NX, NZ, 2, ROWS, COLS), bf16),
        V((2, 2, NY, 8, 128), bf16),
        V((2, 128, 128), bf16),
        V((NX, NZ, 2, 2, ROWS, 128), bf16),
        V((NX, 8, WIN), bf16),
        V((NZ, 2, PACKED, NY, 8, 128), bf16),
        msg, msg, msg, msg, msg, msg,
        V((4 * TOK, 2 * CW), f32),
        V((4, TOK, CW), f32),
        V((CHUNKS, TOK, CW), f32),
        V((8, 256, 256), bf16),
        V((8, 256, 256), bf16),
        V((8, TOK, 256), f32),
        D((4,)), D((8,)),
        D((2, 4)), D((8,)), D((2, 4)), D((3, 4)), D((4,)), D((CHUNKS,)), D((CHUNKS,)),
        D((3,)), D((3,)), D((3,)), D((3,)), D((3,)), D((3,)), D((2, 4)), D((8,)), D((8,)), D((8,)),
        D((3,)), D((3,)), D((3,)), D((3,)), D((2, 4)), D((8, 2)), D((8,)), D((8,)),
        D((3, CHUNKS)), D((3, CHUNKS)),
    ]
    return pl.pallas_call(
        kernel,
        out_shape=jax.ShapeDtypeStruct((TOK, WIN), f32),
        in_specs=[pl.BlockSpec(memory_space=pl.ANY)] * 4,
        out_specs=pl.BlockSpec(memory_space=pl.ANY),
        scratch_shapes=scratch,
        name="whiten",
        compiler_params=pltpu.CompilerParams(
            collective_id=0, has_side_effects=True, vmem_limit_bytes=56 * 2**20
        ),
    )(earlier, window_x, off_block, diag_block)


def solution(mesh):
    return jax.shard_map(
        local,
        mesh=mesh,
        in_specs=(
            P("tok", "feat"),
            P(("tok", "feat"), None),
            P("tok", "feat"),
            P(("tok", "feat"), None),
        ),
        out_specs=P(("tok", "feat"), None),
        check_vma=False,
    )
```

```python
import jax
import jax.numpy as jnp
from jax import lax
from jax.experimental import pallas as pl
from jax.experimental.pallas import tpu as pltpu
from jax.sharding import PartitionSpec as P

f32, bf16 = jnp.float32, jnp.bfloat16
NX, NY, NZ = 4, 4, 8
WIN, COLS, ROWS, TOK = 2048, 1536, 32, 256
CHUNKS, CW = 16, 128
TICKS, LAG = 9, 3
FLOOR = 2.0**-10


def split(v):
    high = v.astype(bf16)
    return high, (v - high.astype(f32)).astype(bf16)


def dot(a, b):
    return lax.dot_general(a, b, (((1,), (0,)), ((), ())), preferred_element_type=f32)


def dot_t(a, b):
    return lax.dot_general(a, b, (((1,), (1,)), ((), ())), preferred_element_type=f32)


def encode(v):
    m = jnp.abs(v) + FLOOR
    m2 = m * m
    m4 = m2 * m2
    m12 = m4 * m4 * m4
    return jnp.where(v < 0, -m12, m12).astype(bf16)


def decode(code):
    c = code.astype(f32)
    m = jnp.exp(jnp.log(jnp.abs(c)) * (1.0 / 12.0)) - FLOOR
    return jnp.where(c < 0, -m, m)


def inverse(block):
    n = block.shape[0]
    r = lax.broadcasted_iota(jnp.int32, (n, n), 0)
    c = lax.broadcasted_iota(jnp.int32, (n, n), 1)
    differ = r ^ c
    x = jnp.where(differ == 0, 1.0 / jnp.where(differ == 0, block, 1.0), 0.0)
    s = 1
    while s < n:
        below = jnp.where((differ >= s) & (differ < 2 * s), block, 0.0).astype(bf16)
        xh, xl = split(x)
        th, tl = split(dot(xh, below) + dot(xl, below))
        x = x - (dot(th, xh) + (dot(th, xl) + dot(tl, xh)))
        s *= 2
    return x


FIRST = (0, 3, 10, 21)
PACKED, HALF = 36, 18


def kernel(e_hbm, x_hbm, w_hbm, dg_hbm, out_hbm, e, xw, dg, ov, wb, gb, iv, vb, lx, lp, hs, si, sd, hr, gi, gd, pb, pk, rem, ih, il, acc,
           in_s, out_s, wz_s, wz_r, wx_s, wx_r, wf_s, ws_s, ws_r, gy_s, gy_r, gg_s, gg_r, vx_s, vx_r, vz_s, vz_r, vt_s, vt_r,
           lx_s, lx_r, ly_s, ly_r, lz_s, lz_r, lt_s, lt_r, rs_s, rs_r):
    t, y = lax.axis_index("tok"), lax.axis_index("feat")
    x, z, c = lax.div(t, 16), lax.rem(lax.div(t, 2), 8), lax.rem(t, 2)
    low = lax.rem(z, 2)

    def at(dx=0, dy=0, dz=0, dc=0):
        xx, yy = lax.rem(x + dx + NX, NX), lax.rem(y + dy + NY, NY)
        zz, cc = lax.rem(z + dz + NZ, NZ), lax.rem(c + dc, 2)
        return (xx * 16 + zz * 2 + cc, yy)

    def copy(src, ss, rs, device, dst=None):
        return pltpu.make_async_remote_copy(
            src_ref=src, dst_ref=src if dst is None else dst, send_sem=ss, recv_sem=rs,
            device_id=device, device_id_type=pl.DeviceIdType.MESH)

    load_w = pltpu.make_async_copy(w_hbm, wb.at[x, z, c], in_s.at[0])
    load_dg = pltpu.make_async_copy(dg_hbm, dg, in_s.at[1])
    load_e = pltpu.make_async_copy(e_hbm, e, in_s.at[2])
    load_x = pltpu.make_async_copy(x_hbm, xw, in_s.at[3])
    for load in (load_w, load_dg, load_e, load_x):
        load.start()

    east, west, up, down, twin = at(dx=1), at(dx=-1), at(dz=1), at(dz=-1), at(dc=1)
    mates = [twin, at(dz=1 - 2 * low), at(dz=1 - 2 * low, dc=1)]
    sides = [at(dx=d) for d in (1, 2, 3)]
    others = [at(dy=d) for d in (1, 2, 3)]

    barrier = pltpu.get_barrier_semaphore()
    partners = [up, down, twin, mates[2], *sides, *others]
    for p in partners:
        pl.semaphore_signal(barrier, inc=1, device_id=p, device_id_type=pl.DeviceIdType.MESH)
    pl.semaphore_wait(barrier, len(partners))

    sg = 2 * low - 1

    def pair_of(k):
        off = jnp.where(k == 0, 0, jnp.where(k == 1, sg, jnp.where(k == 2, -sg, 2)))
        return lax.rem(lax.div(z, 2) + off + 4, 4)

    def chunk_of(n):
        side, g = lax.rem(n, 2), lax.div(n, 2)
        own = jnp.logical_or(g == 0, g == 3)
        far = g >= 6
        near_k = jnp.where(g < 3, g - 1, g - 2)
        k = jnp.where(own, jnp.where(g == 0, side, 2 + side), jnp.where(far, n - 12, near_k))
        xs = jnp.where(own, x, jnp.where(far, x + 2, x + 3 + 2 * side))
        return lax.rem(xs, NX), pair_of(k)

    def rows_of(xs, pair, core):
        return wb.at[xs, pl.ds(2 * pair, 2), core]

    def w_ring(k, zsrc, way):
        return copy(wb.at[x, zsrc, c], wz_s.at[way, k], wz_r.at[zsrc], up if way == 0 else down)

    def w_side(k, way):
        return copy(rows_of(x, pair_of(k), c), wx_s.at[way, k], wx_r.at[way, k], east if way == 0 else west)

    def w_near(k, side):
        return copy(rows_of(lax.rem(x + 3 + 2 * side, NX), pair_of(k), c), wf_s.at[k], wx_r.at[side, k], twin)

    def w_on(k):
        side = k % 2
        return copy(rows_of(lax.rem(x + 3 + 2 * side, NX), pair_of(k), c), wf_s.at[k], wx_r.at[2, k], (east, west)[side])

    def w_far(k):
        return copy(rows_of(lax.rem(x + 2, NX), pair_of(k), c), wf_s.at[k], wx_r.at[2, k], twin)

    def w_twin(n, core):
        xs, pair = chunk_of(n)
        return copy(rows_of(xs, pair, core), ws_s.at[n], ws_r.at[n], twin)

    def own_step(k):
        zm, zp = lax.rem(z - (k + 1) + NZ, NZ), lax.rem(z + k + 1, NZ)
        w_ring(0, zm, 0).wait_recv()
        if k < 3:
            w_ring(k + 1, zm, 0).start()
            w_ring(0, zp, 1).wait_recv()
        if k < 2:
            w_ring(k + 1, zp, 1).start()
        w_twin(jnp.int32((0, 1, 6, 7)[k]), c).start()
        w_side(k, 0).start()
        w_side(k, 1).start()

    def near_step(k):
        for side in (0, 1):
            w_near(k, side).wait_recv()
            if side == k % 2:
                w_on(k).start()
            w_twin(jnp.int32((2, 4, 8, 10)[k] + side), c).start()

    def far_step(k):
        w_far(k).wait_recv()
        w_twin(jnp.int32(12 + k), c).start()

    def g_y(d, yy):
        return copy(gb.at[low, c, yy], gy_s.at[d], gy_r.at[d], others[d])

    def g_mate(i, zl, core):
        return copy(gb.at[zl, core], gg_s.at[i], gg_r.at[i], mates[i])

    def v_x(d, xx):
        return copy(vb.at[xx, z, c], vx_s.at[d], vx_r.at[d], sides[d])

    def v_ring(k, zsrc, way):
        return copy(vb.at[:, zsrc, c], vz_s.at[way, k], vz_r.at[zsrc], up if way == 0 else down)

    def v_twin(zsrc, core):
        return copy(vb.at[:, zsrc, core], vt_s.at[zsrc], vt_r.at[zsrc], twin)

    def invert():
        g_mate(0, low, 1 - c).wait_recv()
        g_mate(1, 1 - low, c).wait_recv()
        g_mate(2, 1 - low, 1 - c).wait_recv()
        iv[0], iv[1] = split(inverse(gb[...].reshape(128, 128).astype(f32)))
        mine = pl.ds(pl.multiple_of(32 * (2 * low + c), 32), 32)
        vb[x, z, c, 0] = iv[0, mine]
        vb[x, z, c, 1] = iv[1, mine]
        for d in range(3):
            v_x(d, x).start()

    def v_step(k):
        if k == 0:
            for d in range(3):
                v_x(d, lax.rem(x + 3 - d, NX)).wait_recv()
            v_ring(0, z, 0).start()
            v_ring(0, z, 1).start()
            v_twin(z, c).start()
            return
        zm, zp = lax.rem(z - k + NZ, NZ), lax.rem(z + k, NZ)
        v_ring(0, zm, 0).wait_recv()
        if k < 4:
            v_ring(k, zm, 0).start()
            v_ring(0, zp, 1).wait_recv()
            if k < 3:
                v_ring(k, zp, 1).start()
            v_twin(zp, c).start()
        v_twin(zm, c).start()

    def l_x(d, xx):
        return copy(lx.at[xx], lx_s.at[d], lx_r.at[d], sides[d])

    def l_pack():
        for xb in range(NX):
            for b in range(4 * xb + 3):
                lp[z, c, FIRST[xb] + b, y] = lx[xb, :, 128 * b : 128 * b + 128]

    def l_y(d, yy):
        return copy(lp.at[z, c, :, yy], ly_s.at[d], ly_r.at[d], others[d])

    def l_ring(k, zsrc, way):
        return copy(lp.at[zsrc, c], lz_s.at[way, k], lz_r.at[zsrc, 0], up if way == 0 else down)

    def l_last(zsrc, way):
        half = lp.at[zsrc, c, pl.ds(HALF * way, HALF)]
        return copy(half, lz_s.at[way, 3], lz_r.at[zsrc, way], up if way == 0 else down)

    def l_twin(zsrc, core):
        return copy(lp.at[zsrc, core], lt_s.at[zsrc], lt_r.at[zsrc], twin)

    def l_step(k):
        if k == 0:
            for d in range(3):
                l_y(d, lax.rem(y + 3 - d, NY)).wait_recv()
            l_ring(0, z, 0).start()
            l_ring(0, z, 1).start()
            l_twin(z, c).start()
            return
        zm, zp = lax.rem(z - k + NZ, NZ), lax.rem(z + k, NZ)
        if k == 4:
            l_last(zm, 0).wait_recv()
            l_last(zm, 1).wait_recv()
            l_twin(zm, c).start()
            return
        for zsrc, way in ((zm, 0), (zp, 1)):
            l_ring(0, zsrc, way).wait_recv()
            if k < 3:
                l_ring(k, zsrc, way).start()
            else:
                l_last(zsrc, way).start()
            l_twin(zsrc, c).start()

    half = lax.div(z, 4)

    def join(far):
        side = 1 - half if far else half
        for i in range(4):
            v_twin(4 * side + i, 1 - c).wait_recv()
            l_twin(4 * side + i, 1 - c).wait_recv()
        for xb in range(NX):
            j = 2 * xb + side
            a, d = pl.ds(4 * side, 2), pl.ds(4 * side + 2, 2)
            ah, al = (vb[xb, a, :, h].reshape(128, 128) for h in (0, 1))
            dh, dl = (vb[xb, d, :, h].reshape(128, 128) for h in (0, 1))
            below = lp[d, :, FIRST[xb] + 2 * j].reshape(128, 128)
            th, tl = split(dot(dh, below) + dot(dl, below))
            bh, bl = split(-(dot(th, ah) + (dot(th, al) + dot(tl, ah))))
            zero = jnp.zeros((128, 128), bf16)
            for ref, parts in ((ih, (ah, zero, bh, dh)), (il, (al, zero, bl, dl))):
                ref[j, :128, :128] = parts[0]
                ref[j, :128, 128:] = parts[1]
                ref[j, 128:, :128] = parts[2]
                ref[j, 128:, 128:] = parts[3]

    def sent():
        for k in range(4):
            w_ring(k, z, 0).wait_send()
            if k < 3:
                w_ring(k, z, 1).wait_send()
            w_side(k, 0).wait_send()
            w_side(k, 1).wait_send()
            w_on(k).wait_send()
        for n in range(CHUNKS):
            w_twin(n, c).wait_send()
        for d in range(3):
            for cp in (g_y(d, y), g_mate(d, low, c), v_x(d, x), l_x(d, x), l_y(d, y)):
                cp.wait_send()
        for k in range(4):
            v_ring(k, z, 0).wait_send()
            if k < 3:
                v_ring(k, z, 1).wait_send()
        for k in range(3):
            l_ring(k, z, 0).wait_send()
            l_ring(k, z, 1).wait_send()
        l_last(z, 0).wait_send()
        l_last(z, 1).wait_send()
        for zz in range(NZ):
            v_twin(zz, c).wait_send()
            l_twin(zz, c).wait_send()

    def at_tick(tick, steps):
        for when, do in steps.items():

            @pl.when(tick == when)
            def _(do=do):
                for f, *k in do:
                    f(*k)

    def toward(n):
        return lax.rem(y + 1 + 2 * lax.rem(n, 2), NY)

    def share(kind, n):
        to = toward(n) if kind != 1 else lax.rem(toward(n) + 2, NY)
        src, dst = ((hs, hr), (si, gi), (sd, gd))[kind]
        return copy(src.at[n], rs_s.at[kind, n], rs_r.at[kind, n], (t, to), dst.at[n])

    def rows(n):
        xs, pair = chunk_of(n)
        w_twin(n, 1 - c).wait_recv()
        return wb[xs, pl.ds(2 * pair, 2)].reshape(CW, COLS)

    def hand_out(n, i):
        def part(d):
            return pb[pl.ds(pl.multiple_of(d * TOK, TOK), TOK), pl.ds(CW * i, CW)]

        nd = toward(n)
        hs[n] = encode(part(lax.rem(y + 2, NY)))
        share(0, n).start()
        si[n] = encode(part(lax.rem(nd + 2, NY)))
        share(1, n).start()
        pk[lax.rem(n, 4)] = part(nd)
        xs, pair = chunk_of(n)
        q = 4 * xs + pair
        rem[q] = xw[:, pl.ds(pl.multiple_of(q * CW, CW), CW)].astype(f32) - part(y)

    def pass_on(n):
        share(0, n).wait_recv()
        sd[n] = encode(pk[lax.rem(n, 4)] + decode(hr[n]))
        share(2, n).start()

    def finish(n):
        xs, pair = chunk_of(n)
        q = 4 * xs + pair
        share(1, n).wait_recv()
        share(2, n).wait_recv()
        for kind in range(3):
            share(kind, n).wait_send()
        rem[q] = rem[q] - (decode(gi[n]) + decode(gd[n]))

    def each(tick, do):
        n = jnp.where(tick < 2, tick, 2 * tick - 2)
        do(n)

        @pl.when(tick >= 2)
        def _():
            do(n + 1)

    load_w.wait()
    w_ring(0, z, 0).start()
    w_ring(0, z, 1).start()
    load_dg.wait()
    lx[x] = dg[...]
    gb[low, c, y] = dg[:, pl.ds(pl.multiple_of(lax.div(t, 4) * 128, 128), 128)]
    for d in range(3):
        g_y(d, y).start()
    for d in range(3):
        l_x(d, x).start()
    own_step(0)
    for d in range(3):
        g_y(d, lax.rem(y + 3 - d, NY)).wait_recv()
    for i in range(3):
        g_mate(i, low, c).start()
    for d in range(3):
        l_x(d, lax.rem(x + 3 - d, NX)).wait_recv()
    l_pack()
    for d in range(3):
        l_y(d, y).start()
    load_e.wait()
    load_x.wait()

    @pl.loop(0, TICKS + LAG)
    def _(tick):
        @pl.when(tick < 2)
        def _():
            pb[:, pl.ds(0, CW)] = dot_t(e[...], rows(tick))
            hand_out(tick, 0)

        @pl.when(jnp.logical_and(tick >= 2, tick < TICKS))
        def _():
            n = 2 * tick - 2
            pb[...] = dot_t(e[...], jnp.concatenate([rows(n), rows(n + 1)], axis=0))
            hand_out(n, 0)
            hand_out(n + 1, 1)

        at_tick(tick, {
            0: [(own_step, 1)],
            1: [(own_step, 2), (l_step, 0)],
            2: [(near_step, 1)],
            4: [(l_step, 1), (far_step, 0), (near_step, 2), (v_step, 1)],
            5: [(near_step, 3)],
            6: [(far_step, 2)],
            7: [(l_step, 3)],
            8: [(v_step, 3)],
            9: [(v_step, 4)],
        })

        @pl.when(jnp.logical_and(tick >= 1, tick <= TICKS))
        def _():
            each(tick - 1, pass_on)

        @pl.when(tick >= LAG)
        def _():
            each(tick - LAG, finish)

        at_tick(tick, {
            0: [(invert,), (near_step, 0)],
            2: [(v_step, 0), (own_step, 3)],
            4: [(far_step, 1)],
            5: [(l_step, 2)],
            6: [(far_step, 3), (v_step, 2)],
            8: [(l_step, 4), (join, False)],
            9: [(join, True)],
        })

    def store(j):
        return pltpu.make_async_copy(ov.at[j], out_hbm.at[:, pl.ds(256 * j, 256)], out_s.at[j])

    for j in range(8):
        v = jnp.concatenate([rem[2 * j], rem[2 * j + 1]], axis=1)
        if j:
            v = v - acc[j]
        vh, vl = split(v)
        o = dot_t(vh, ih[j]) + (dot_t(vh, il[j]) + dot_t(vl, ih[j]))
        ov[j] = o
        store(j).start()
        oh, ol = split(o)
        for i in range(j + 1, 8):
            at_z, first = pl.ds(4 * (i % 2), 4), FIRST[i // 2] + 2 * j
            block = jnp.concatenate([lp[at_z, :, first + b].reshape(256, 128) for b in (0, 1)], axis=1)
            u = dot_t(oh, block) + dot_t(ol, block)
            acc[i] = u if j == 0 else acc[i] + u

    sent()
    for j in range(8):
        store(j).wait()


def local(earlier, window_x, off_block, diag_block):
    V, D = pltpu.VMEM, pltpu.SemaphoreType.DMA
    msg = V((CHUNKS, TOK, CW), bf16)
    scratch = [
        V((4 * TOK, COLS), bf16),
        V((TOK, WIN), bf16),
        V((8, WIN), bf16),
        V((8, TOK, 256), f32),
        V((NX, NZ, 2, ROWS, COLS), bf16),
        V((2, 2, NY, 8, 128), bf16),
        V((2, 128, 128), bf16),
        V((NX, NZ, 2, 2, ROWS, 128), bf16),
        V((NX, 8, WIN), bf16),
        V((NZ, 2, PACKED, NY, 8, 128), bf16),
        msg, msg, msg, msg, msg, msg,
        V((4 * TOK, 2 * CW), f32),
        V((4, TOK, CW), f32),
        V((CHUNKS, TOK, CW), f32),
        V((8, 256, 256), bf16),
        V((8, 256, 256), bf16),
        V((8, TOK, 256), f32),
        D((4,)), D((8,)),
        D((2, 4)), D((8,)), D((2, 4)), D((3, 4)), D((4,)), D((CHUNKS,)), D((CHUNKS,)),
        D((3,)), D((3,)), D((3,)), D((3,)), D((3,)), D((3,)), D((2, 4)), D((8,)), D((8,)), D((8,)),
        D((3,)), D((3,)), D((3,)), D((3,)), D((2, 4)), D((8, 2)), D((8,)), D((8,)),
        D((3, CHUNKS)), D((3, CHUNKS)),
    ]
    return pl.pallas_call(
        kernel,
        out_shape=jax.ShapeDtypeStruct((TOK, WIN), f32),
        in_specs=[pl.BlockSpec(memory_space=pl.ANY)] * 4,
        out_specs=pl.BlockSpec(memory_space=pl.ANY),
        scratch_shapes=scratch,
        name="whiten",
        compiler_params=pltpu.CompilerParams(
            collective_id=0, has_side_effects=True, vmem_limit_bytes=56 * 2**20
        ),
    )(earlier, window_x, off_block, diag_block)


def solution(mesh):
    return jax.shard_map(
        local,
        mesh=mesh,
        in_specs=(
            P("tok", "feat"),
            P(("tok", "feat"), None),
            P("tok", "feat"),
            P(("tok", "feat"), None),
        ),
        out_specs=P(("tok", "feat"), None),
        check_vma=False,
    )
```
